256 devices in a mesh: ctx: 32 (over z, y), mp: 8 (over x, core).
Axes of the slice: x: 4, y: 4, z: 8, core: 2. Of those that a mesh axis runs over, the one named last changes fastest.
Arguments:
- query_rows: bfloat16 [16384, 4096], P('ctx', 'mp'), may hold values from -6 to 6
- key_rows: bfloat16 [16384, 4096], P('ctx', 'mp'), may hold values from -6 to 6
- value_rows: bfloat16 [16384, 4096], P('ctx', 'mp'), may hold values from -6 to 6
- out_weight: bfloat16 [4096, 4096], P('mp'), may hold values from -0.375 to 0.375
- random_ids: int32 [128, 3], P('ctx'), may hold values from 0 to 127, as said below
- global_ids: int32 [2], replicated, may hold values from 0 to 127, as said below
Outputs:
- projected: bfloat16 [16384, 4096], P(('ctx', 'mp'))
The draws below stay inside these ranges and needn't reach their ends.
Inputs may be any that keep to these rules, and one draw needn't show every extreme that they name: `random_ids`: take the 4 query blocks of one index of ctx and the aligned group of 4 key blocks of any one index of ctx: at most 2 of those query blocks' random ids (counted with repeats) fall in that group, and exactly 2 fall in some group in every draw. `global_ids`: two different block ids, one of them the document's last block.
All inputs are finite; a program needn't handle non-finite values.
Results may differ from the reference program's by a relative error of at most 0.02.
Values may be sent and summed in bfloat16 or wider, within the bound.
A program may use at most 128 MiB of HBM per device.

```python
import math
import jax
import jax.numpy as jnp
from jax import lax

D = 4096
HEADS = 32
HD = 128
BLK = 128
RAND = 3
GLOB = 2
QB_DEV = 4
TOKENS = 16384
NB = 128
MOST = 2
N_CTX = 32
N_MP = 8


def draw_query_rows(key, part):
    key = jax.random.fold_in(key, 3)
    return jax.random.truncated_normal(key, -6.0, 6.0, (TOKENS, HEADS * HD), jnp.float32).astype(jnp.bfloat16)


def draw_key_rows(key, part):
    key = jax.random.fold_in(key, 4)
    return jax.random.truncated_normal(key, -6.0, 6.0, (TOKENS, HEADS * HD), jnp.float32).astype(jnp.bfloat16)


def draw_random_ids(key, part):
    key = jax.random.fold_in(key, 7)
    level_key, forced_key, device_key = jax.random.split(key, 3)
    levels = jax.random.randint(level_key, (N_CTX,), 0, 2)
    forced = jax.random.randint(forced_key, (), 0, N_CTX)
    levels = jnp.where(jnp.arange(N_CTX) == forced, 2, levels).astype(jnp.int32)
    slot_owner = jnp.repeat(jnp.arange(N_CTX, dtype=jnp.int32), MOST)
    request_count = QB_DEV * RAND
    slot_total = N_CTX * MOST

    def one_device(device_seed):
        score_key, shuffle_key, local_key = jax.random.split(device_seed, 3)
        scores = jax.random.randint(score_key, (slot_total,), 0, 2 ** 20) + levels[slot_owner] * 2 ** 20
        scores = scores * slot_total + jnp.arange(slot_total, dtype=jnp.int32)
        chosen = slot_owner[jnp.argsort(-scores)[:request_count]]
        chosen = jax.random.permutation(shuffle_key, chosen)
        local_blocks = jax.random.randint(local_key, (request_count,), 0, QB_DEV)
        return (chosen * QB_DEV + local_blocks).reshape(QB_DEV, RAND)
    chosen_ids = jax.vmap(one_device)(jax.random.split(device_key, N_CTX))
    return chosen_ids.reshape(NB, RAND).astype(jnp.int32)


def draw_global_ids(key, part):
    key = jax.random.fold_in(key, 9)
    first_key, order_key = jax.random.split(key)
    other_id = jax.random.randint(first_key, (), 0, NB - 1)
    last_id = jnp.int32(NB - 1)
    swapped = jax.random.randint(order_key, (), 0, 2)
    first_id = jnp.where(swapped == 1, last_id, other_id)
    second_id = jnp.where(swapped == 1, other_id, last_id)
    return jnp.stack([first_id, second_id]).astype(jnp.int32)


def block_levels(own_key, dims, pieces, smallest, largest):
    loudness = 1.0
    for position, blocks in pieces:
        steps = jax.random.uniform(jax.random.fold_in(jax.random.fold_in(own_key, 6), position), (blocks,), jnp.float32, smallest / len(pieces), largest / len(pieces))
        loudness = loudness * jnp.repeat(jnp.exp(steps), dims[position] // blocks).reshape((-1,) + (1,) * (len(dims) - 1 - position))
    return loudness


def centred(own_key, shape, width, most, cuts=(), kind=jnp.bfloat16):
    loudness = block_levels(own_key, shape, cuts, -0.22, 0.18) if cuts else 1.0
    result = jax.random.normal(own_key, shape, jnp.float32) * width * loudness
    return jnp.minimum(jnp.maximum(result, -most), most).astype(kind)


def setup_inputs(seed: int = 0) -> dict:
    arg_keys = jax.random.split(jax.random.key(seed), 7)
    return {
        "query_rows": draw_query_rows(jax.random.fold_in(arg_keys[6], 71), 0),
        "key_rows": draw_key_rows(jax.random.fold_in(arg_keys[6], 71), 0),
        "value_rows": centred(arg_keys[2], (TOKENS, HEADS * HD), 1.0, 6.0, ((0, 32), (1, 8))),
        "out_weight": centred(arg_keys[3], (HEADS * HD, D), (HEADS * HD // 16) ** -0.5, 0.375, ((0, 8),)),
        "random_ids": draw_random_ids(jax.random.fold_in(arg_keys[6], 71), 0),
        "global_ids": draw_global_ids(jax.random.fold_in(arg_keys[6], 71), 0),
    }


def block_attend(query_block, pair_block):
    features = query_block.shape[-1]
    head_count = features // HD
    query_heads = query_block.reshape(BLK, head_count, HD).astype(jnp.float32)
    key_heads = pair_block[:, 0, :].reshape(BLK, head_count, HD).astype(jnp.float32)
    value_heads = pair_block[:, 1, :].reshape(BLK, head_count, HD).astype(jnp.float32)
    scores = jnp.einsum('qhd,khd->hqk', query_heads, key_heads) * (1.0 / math.sqrt(HD))
    maxima = lax.optimization_barrier(jnp.max(scores, axis=-1))
    weights = jnp.exp(scores - maxima[..., None]).astype(jnp.bfloat16)
    totals = lax.optimization_barrier(jnp.sum(weights.astype(jnp.float32), axis=-1))
    outputs = jnp.einsum('hqk,khd->qhd', weights.astype(jnp.float32), value_heads)
    return (outputs, maxima, totals)

def reference(query_rows, key_rows, value_rows, out_weight, random_ids, global_ids):
    features = query_rows.shape[1]
    head_count = features // HD
    query_blocks = query_rows.reshape(NB, BLK, features)
    pair_blocks = jnp.stack([key_rows, value_rows], axis=1).reshape(NB, BLK, 2, features)

    def one_block(current):
        previous = current - 1
        following = current + 1
        listed = jnp.concatenate([jnp.stack([previous, current, following]).astype(jnp.int32), global_ids.astype(jnp.int32), random_ids[current].astype(jnp.int32)])
        usable = jnp.concatenate([jnp.stack([previous >= 0, current >= 0, following < NB]), jnp.ones((GLOB + RAND,), jnp.bool_)])
        clipped = jnp.clip(listed, 0, NB - 1).astype(jnp.int32)
        outputs, maxima, totals = jax.vmap(block_attend, in_axes=(None, 0))(query_blocks[current], pair_blocks[clipped])
        highest = lax.optimization_barrier(jnp.max(jnp.where(usable[:, None, None], maxima, jnp.float32(-1e+30)), axis=0))
        scales = jnp.where(usable[:, None, None], jnp.exp(maxima - highest[None]), jnp.float32(0.0))
        numerator = lax.optimization_barrier(jnp.sum(outputs * jnp.transpose(scales, (0, 2, 1))[..., None], axis=0))
        denominator = lax.optimization_barrier(jnp.sum(scales * totals, axis=0))
        return (numerator / jnp.transpose(denominator)[..., None]).reshape(BLK, features).astype(jnp.bfloat16)
    attended = lax.map(one_block, jnp.arange(NB, dtype=jnp.int32)).reshape(NB * BLK, features)
    columns = features // N_MP
    projected = jnp.zeros((NB * BLK, out_weight.shape[1]), jnp.float32)
    for segment in range(N_MP):
        head_term = jnp.dot(attended[:, segment * columns:(segment + 1) * columns], out_weight[segment * columns:(segment + 1) * columns], preferred_element_type=jnp.float32)
        head_term = lax.optimization_barrier(head_term.astype(jnp.bfloat16))
        projected = projected + head_term.astype(jnp.float32)
    return projected.astype(jnp.bfloat16)
```

```python
import math

import jax
import jax.numpy as jnp
from jax import lax
from jax.experimental import pallas as pl
from jax.experimental.pallas import tpu as pltpu
from jax.sharding import PartitionSpec as P

HD = 128
BLK = 128
RAND = 3
GLOB = 2
NZ = 8
NY = 4
NX = 4
HEADS = 4
QB = 4
ROWS = QB * BLK
FEATS = HEADS * HD
WIDTH = 4096
HALF = BLK // 2
SCALE = 1.0 / math.sqrt(HD)
LOW = -1e30
MESH = pl.DeviceIdType.MESH
NT = (((1,), (1,)), ((), ()))
TN = (((0,), (0,)), ((), ()))
RING = 14
MIB = 1024 * 1024


def any_spec():
    return pl.BlockSpec(memory_space=pl.ANY)


def vmem_spec():
    return pl.BlockSpec(memory_space=pltpu.VMEM)


def smem_spec():
    return pl.BlockSpec(memory_space=pltpu.SMEM)


def places():
    me = lax.axis_index("ctx")
    mp = lax.axis_index("mp")
    return me, me // NY, me % NY, mp, mp // 2, mp % 2


def gather_kernel(
    q_ref, k_ref, v_ref, w_ref, ids_ref,
    kcol, vcol, qrow, idrow, wsib, acc_out, stat_out,
    q_own, k_ext, v_ext,
    ring_send, ring_recv, row_send, row_recv, edge_send, edge_recv, w_sem, local_sem,
):
    me, z, y, mp, x, core = places()
    count = NZ * NY
    after, before = (me + 1) % count, (me + count - 1) % count
    sibling = mp + 1 - 2 * core
    up, down = (z + 1) % NZ, (z + NZ - 1) % NZ

    barrier = pltpu.get_barrier_semaphore()
    peers = [{"ctx": up * NY + y}, {"ctx": down * NY + y}]
    peers += [{"ctx": z * NY + (y + d) % NY} for d in range(1, NY)]
    peers += [{"ctx": after}, {"ctx": before}, {"mp": sibling}]
    for peer in peers:
        pl.semaphore_signal(barrier, inc=1, device_id=peer, device_id_type=MESH)
    pl.semaphore_wait(barrier, len(peers))

    def remote(src, dst, send, recv, peer):
        return pltpu.make_async_remote_copy(
            src_ref=src, dst_ref=dst, send_sem=send, recv_sem=recv, device_id=peer, device_id_type=MESH
        )

    edges = []
    for n, (own, ext) in enumerate(((k_ref, k_ext), (v_ref, v_ext))):
        edges.append(remote(own.at[pl.ds(ROWS - BLK, BLK)], ext.at[pl.ds(0, BLK)],
                            edge_send.at[2 * n], edge_recv.at[2 * n], {"ctx": after}))
        edges.append(remote(own.at[pl.ds(0, BLK)], ext.at[pl.ds(ROWS + BLK, BLK)],
                            edge_send.at[2 * n + 1], edge_recv.at[2 * n + 1], {"ctx": before}))

    def ring(way, i):
        sign = 1 if way == 0 else -1
        back, piece = i // 4, i % 4
        source = (z + NZ - sign * back) % NZ
        is_key = (piece < 2) == (way == 0)
        own, col = (k_ref, kcol) if is_key else (v_ref, vcol)
        rows = pl.ds((piece % 2) * (ROWS // 2), ROWS // 2)
        src = own.at[rows] if back == 0 else col.at[source, rows]
        peer = {"ctx": (up if way == 0 else down) * NY + y}
        return remote(src, col.at[source, rows], ring_send.at[way, i], ring_recv.at[way, i], peer)

    rings = [[ring(way, i) for i in range(RING)] for way in range(2)]
    rows = []
    for d in range(1, NY):
        peer = {"ctx": z * NY + (y + d) % NY}
        rows.append(remote(ids_ref, idrow.at[y], row_send.at[1, d - 1], row_recv.at[1, d - 1], peer))
        rows.append(remote(q_ref, qrow.at[y], row_send.at[0, d - 1], row_recv.at[0, d - 1], peer))
    weight = remote(w_ref, wsib, w_sem.at[0], w_sem.at[1], {"mp": sibling})

    for copy in edges:
        copy.start()
    for i in range(4):
        rings[0][i].start()
        rings[1][i].start()
    local = [
        pltpu.make_async_copy(q_ref, q_own, local_sem.at[0]),
        pltpu.make_async_copy(k_ref, k_ext.at[pl.ds(BLK, ROWS)], local_sem.at[1]),
        pltpu.make_async_copy(v_ref, v_ext.at[pl.ds(BLK, ROWS)], local_sem.at[2]),
        pltpu.make_async_copy(k_ref, kcol.at[z], local_sem.at[3]),
        pltpu.make_async_copy(v_ref, vcol.at[z], local_sem.at[4]),
        pltpu.make_async_copy(q_ref, qrow.at[y], local_sem.at[5]),
        pltpu.make_async_copy(ids_ref, idrow.at[y], local_sem.at[6]),
    ]
    for copy in local:
        copy.start()
    for copy in rows:
        copy.start()
    weight.start()
    for copy in local[:3]:
        copy.wait()
    for copy in edges:
        copy.wait_recv()

    def window(qb):
        row = lax.broadcasted_iota(jnp.int32, (3 * BLK, 1), 0)
        first = jnp.where(me + qb == 0, BLK, 0)
        last = jnp.where(me * QB + qb == count * QB - 1, 2 * BLK, 3 * BLK)
        live = (row >= first) & (row < last)
        span = pl.ds(pl.multiple_of(qb * BLK, BLK), 3 * BLK)
        for h in range(HEADS):
            cols = pl.ds(h * HD, HD)
            q = q_own[pl.ds(pl.multiple_of(qb * BLK, BLK), BLK), cols]
            s = lax.dot_general(k_ext[span, cols], q, NT, preferred_element_type=jnp.float32) * SCALE
            s = jnp.where(live, s, LOW)
            top = jnp.max(s, axis=0, keepdims=True)
            p = jnp.where(live, jnp.exp(s - top), 0.0).astype(jnp.bfloat16)
            stat_out[qb, pl.ds(h, 1), :] = top
            stat_out[qb, pl.ds(HEADS + h, 1), :] = jnp.sum(p.astype(jnp.float32), axis=0, keepdims=True)
            acc_out[qb, cols, :] = lax.dot_general(v_ext[span, cols], p, TN, preferred_element_type=jnp.float32)

    for i in range(RING):
        if i < QB:
            window(i)
        for way in range(2):
            rings[way][i].wait_recv()
            if i + 4 < RING:
                rings[way][i + 4].start()
    for copy in local[3:]:
        copy.wait()
    for copy in edges:
        copy.wait_send()
    for way in range(2):
        for i in range(RING):
            rings[way][i].wait_send()
    for copy in rows:
        copy.wait()
    weight.wait()


def gather(q, k, v, w, ids):
    bf, f32 = jnp.bfloat16, jnp.float32
    dma = pltpu.SemaphoreType.DMA
    return pl.pallas_call(
        gather_kernel,
        name="gather_and_window",
        out_shape=(
            jax.ShapeDtypeStruct((NZ, ROWS, FEATS), bf),
            jax.ShapeDtypeStruct((NZ, ROWS, FEATS), bf),
            jax.ShapeDtypeStruct((NY, ROWS, FEATS), bf),
            jax.ShapeDtypeStruct((NY, 8, 128), jnp.int32),
            jax.ShapeDtypeStruct((FEATS, WIDTH), bf),
            jax.ShapeDtypeStruct((QB, FEATS, BLK), f32),
            jax.ShapeDtypeStruct((QB, 2 * HEADS, BLK), f32),
        ),
        in_specs=[any_spec()] * 5,
        out_specs=(any_spec(),) * 5 + (vmem_spec(), vmem_spec()),
        scratch_shapes=[
            pltpu.VMEM((ROWS, FEATS), bf),
            pltpu.VMEM((ROWS + 2 * BLK, FEATS), bf),
            pltpu.VMEM((ROWS + 2 * BLK, FEATS), bf),
            dma((2, RING)), dma((2, RING)), dma((2, NY - 1)), dma((2, NY - 1)),
            dma((4,)), dma((4,)), dma((2,)), dma((7,)),
        ],
        compiler_params=pltpu.CompilerParams(
            collective_id=0, has_side_effects=True, vmem_limit_bytes=24 * MIB
        ),
        cost_estimate=pl.CostEstimate(flops=400 * 10**6, bytes_accessed=24 * MIB, transcendentals=0),
    )(q, k, v, w, ids)


def far_kernel(ids_ref, glob_ref, kcol, vcol, qrow, part_out, stat_out, acc, top_ref, sum_ref):
    y = lax.axis_index("ctx") % NY

    def attend(t, block):
        zs = lax.div(block, NY * QB)
        rows = pl.ds(pl.multiple_of(lax.rem(block, QB) * BLK, BLK), BLK)
        q_rows = pl.ds(pl.multiple_of(lax.rem(t, QB) * BLK, BLK), BLK)
        for h in range(HEADS):
            cols = pl.ds(h * HD, HD)
            q = qrow[lax.div(t, QB), q_rows, cols]
            s = lax.dot_general(kcol[zs, rows, cols], q, NT, preferred_element_type=jnp.float32) * SCALE
            old = top_ref[pl.ds(h, 1), :]
            top = jnp.maximum(old, jnp.max(s, axis=0, keepdims=True))
            p = jnp.exp(s - top).astype(jnp.bfloat16)
            fade = jnp.exp(old - top)
            top_ref[pl.ds(h, 1), :] = top
            sum_ref[pl.ds(h, 1), :] = sum_ref[pl.ds(h, 1), :] * fade + jnp.sum(
                p.astype(jnp.float32), axis=0, keepdims=True)
            acc[cols, :] = acc[cols, :] * fade + lax.dot_general(
                vcol[zs, rows, cols], p, TN, preferred_element_type=jnp.float32)

    def one(t, carry):
        acc[...] = jnp.zeros_like(acc)
        top_ref[...] = jnp.full_like(top_ref, LOW)
        sum_ref[...] = jnp.zeros_like(sum_ref)
        yd, qb = lax.div(t, QB), lax.rem(t, QB)
        for j in range(GLOB + RAND):
            block = glob_ref[j] if j < GLOB else ids_ref[yd, qb, j - GLOB]

            @pl.when(lax.rem(lax.div(block, QB), NY) == y)
            def _():
                attend(t, block)

        for h in range(HEADS):
            cols = pl.ds(h * HD, HD)
            total = sum_ref[pl.ds(h, 1), :]
            part_out[yd, qb, cols, :] = jnp.where(
                total > 0, acc[cols, :] / jnp.where(total > 0, total, 1.0), 0.0).astype(jnp.bfloat16)
            stat_out[yd, qb, pl.ds(h, 1), :] = top_ref[pl.ds(h, 1), :]
            stat_out[yd, qb, pl.ds(HEADS + h, 1), :] = total
        return carry

    lax.fori_loop(0, NY * QB, one, 0)


def far(idrow, globs, kcol, vcol, qrow):
    f32 = jnp.float32
    return pl.pallas_call(
        far_kernel,
        name="random_and_global",
        out_shape=(
            jax.ShapeDtypeStruct((NY, QB, FEATS, BLK), jnp.bfloat16),
            jax.ShapeDtypeStruct((NY, QB, 2 * HEADS, BLK), f32),
        ),
        in_specs=[smem_spec(), smem_spec(), vmem_spec(), vmem_spec(), vmem_spec()],
        out_specs=(vmem_spec(), vmem_spec()),
        scratch_shapes=[
            pltpu.VMEM((FEATS, BLK), f32), pltpu.VMEM((8, BLK), f32), pltpu.VMEM((8, BLK), f32),
        ],
        compiler_params=pltpu.CompilerParams(vmem_limit_bytes=40 * MIB),
        cost_estimate=pl.CostEstimate(flops=800 * 10**6, bytes_accessed=14 * MIB, transcendentals=0),
    )(idrow, globs, kcol, vcol, qrow)


def merge_kernel(
    acc_ref, wstat_ref, part, pstat, w_ref, wsib_ref, out_ref,
    got, got_stat, w_own, w_other, att, att_other, sent, relay, final, total,
    part_send, part_recv, stat_send, stat_recv, att_send, att_recv, x_send, x_recv, local_sem,
):
    me, z, y, mp, x, core = places()
    sibling = mp + 1 - 2 * core
    right, left = ((x + 1) % NX) * 2 + core, ((x + NX - 1) % NX) * 2 + core
    order = [(x + d) % NX for d in (2, 1, 3, 0)]

    barrier = pltpu.get_barrier_semaphore()
    peers = [{"ctx": z * NY + (y + d) % NY} for d in range(1, NY)]
    peers += [{"mp": sibling}, {"mp": right}, {"mp": left}]
    for peer in peers:
        pl.semaphore_signal(barrier, inc=1, device_id=peer, device_id_type=MESH)

    local = [
        pltpu.make_async_copy(part.at[y], got.at[NY - 1], local_sem.at[0]),
        pltpu.make_async_copy(pstat.at[y], got_stat.at[NY - 1], local_sem.at[1]),
        pltpu.make_async_copy(w_ref, w_own, local_sem.at[2]),
        pltpu.make_async_copy(wsib_ref, w_other, local_sem.at[3]),
    ]
    for copy in local:
        copy.start()
    pl.semaphore_wait(barrier, len(peers))

    def remote(src, dst, send, recv, peer):
        return pltpu.make_async_remote_copy(
            src_ref=src, dst_ref=dst, send_sem=send, recv_sem=recv, device_id=peer, device_id_type=MESH
        )

    stats, parts = [], []
    for d in range(1, NY):
        to = (y + d) % NY
        stats.append(remote(pstat.at[to], got_stat.at[d - 1], stat_send.at[d - 1], stat_recv.at[d - 1],
                            {"ctx": z * NY + to}))
        stats[-1].start()
    for i, qb in enumerate(order):
        parts.append([])
        for d in (2, 1, 3):
            to = (y + d) % NY
            parts[-1].append(remote(part.at[to, qb], got.at[d - 1, qb], part_send.at[d - 1, i],
                                    part_recv.at[d - 1, i], {"ctx": z * NY + to}))
            parts[-1][-1].start()
    for copy in stats:
        copy.wait_recv()
    for copy in local:
        copy.wait()

    swaps, sends = [], []
    mine = pl.ds(pl.multiple_of(core * HALF, HALF), HALF)
    theirs = pl.ds(pl.multiple_of((1 - core) * HALF, HALF), HALF)
    tile = 512
    middle = WIDTH // 2
    for i, qb in enumerate(order):
        for copy in parts[i]:
            copy.wait_recv()
        for h in range(HEADS):
            cols = pl.ds(h * HD, HD)
            tops = [wstat_ref[qb, pl.ds(h, 1), :]] + [got_stat[s, qb, pl.ds(h, 1), :] for s in range(NY)]
            sums = [wstat_ref[qb, pl.ds(HEADS + h, 1), :]] + [
                got_stat[s, qb, pl.ds(HEADS + h, 1), :] for s in range(NY)]
            best = tops[0]
            for top in tops[1:]:
                best = jnp.maximum(best, top)
            scales = [jnp.exp(top - best) for top in tops]
            weights = [scale * part_sum for scale, part_sum in zip(scales, sums)]
            low = weights[0] + weights[1] + weights[2] + weights[3] + weights[4]
            value = acc_ref[qb, cols, :] * (scales[0] / low)
            for s in range(NY):
                value += got[s, qb, cols, :].astype(jnp.float32) * (weights[s + 1] / low)
            att[i, :, cols] = value.T.astype(jnp.bfloat16)
        swaps.append(remote(att.at[i, theirs], att_other.at[i], att_send.at[i], att_recv.at[i], {"mp": sibling}))
        swaps[i].start()
        swaps[i].wait_recv()
        if i == 1:
            sends[0].wait_recv()
        if i == 2:
            sends[1].wait_recv()
        if i == 3:
            sends[2].wait_recv()
            sends[3].wait_recv()

        def project(n, carry):
            cols = pl.ds(pl.multiple_of(n * tile, tile), tile)
            value = jnp.dot(att[i, mine, :], w_own[:, cols], preferred_element_type=jnp.float32)
            value += jnp.dot(att_other[i], w_other[:, cols], preferred_element_type=jnp.float32)
            if i == 3:
                value += final[0, :, cols].astype(jnp.float32) + final[1, :, cols].astype(jnp.float32)
                out_ref[:, cols] = value.astype(jnp.bfloat16)
            else:
                total[:, cols] = value
            return carry

        lax.fori_loop(0, WIDTH // tile, project, 0)
        if i == 1:
            total[:, pl.ds(0, middle)] += relay[0].astype(jnp.float32)
        if i == 2:
            total[:, pl.ds(middle, middle)] += relay[1].astype(jnp.float32)
        if i < 3:
            sent[i] = total[...].astype(jnp.bfloat16)
        if i == 0:
            for s, peer in enumerate((right, left)):
                sends.append(remote(sent.at[0, :, pl.ds(s * middle, middle)], relay.at[s],
                                    x_send.at[s], x_recv.at[s], {"mp": peer}))
                sends[-1].start()
        elif i < 3:
            sends.append(remote(sent.at[i], final.at[i - 1], x_send.at[i + 1], x_recv.at[i + 1],
                                {"mp": right if i == 1 else left}))
            sends[-1].start()

    for copy in stats + sends + swaps:
        copy.wait_send()
    for copies in parts:
        for copy in copies:
            copy.wait_send()


def merge(acc, wstat, part, pstat, w, wsib):
    bf, f32 = jnp.bfloat16, jnp.float32
    dma = pltpu.SemaphoreType.DMA
    return pl.pallas_call(
        merge_kernel,
        name="merge_and_project",
        out_shape=jax.ShapeDtypeStruct((HALF, WIDTH), bf),
        in_specs=[vmem_spec(), vmem_spec(), any_spec(), any_spec(), any_spec(), any_spec()],
        out_specs=vmem_spec(),
        scratch_shapes=[
            pltpu.VMEM((NY, QB, FEATS, BLK), bf),
            pltpu.VMEM((NY, QB, 2 * HEADS, BLK), f32),
            pltpu.VMEM((FEATS, WIDTH), bf),
            pltpu.VMEM((FEATS, WIDTH), bf),
            pltpu.VMEM((QB, BLK, FEATS), bf),
            pltpu.VMEM((QB, HALF, FEATS), bf),
            pltpu.VMEM((3, HALF, WIDTH), bf),
            pltpu.VMEM((2, HALF, WIDTH // 2), bf),
            pltpu.VMEM((2, HALF, WIDTH), bf),
            pltpu.VMEM((HALF, WIDTH), f32),
            dma((NY - 1, QB)), dma((NY - 1, QB)), dma((NY - 1,)), dma((NY - 1,)),
            dma((QB,)), dma((QB,)), dma((4,)), dma((4,)), dma((4,)),
        ],
        compiler_params=pltpu.CompilerParams(
            collective_id=1, has_side_effects=True, vmem_limit_bytes=40 * MIB
        ),
        cost_estimate=pl.CostEstimate(flops=2100 * 10**6, bytes_accessed=14 * MIB, transcendentals=0),
    )(acc, wstat, part, pstat, w, wsib)


def shards(query_rows, key_rows, value_rows, out_weight, random_ids, global_ids):
    ids = jnp.pad(random_ids, ((0, 8 - QB), (0, 128 - RAND)))
    kcol, vcol, qrow, idrow, wsib, acc, wstat = gather(query_rows, key_rows, value_rows, out_weight, ids)
    part, pstat = far(idrow, global_ids, kcol, vcol, qrow)
    return merge(acc, wstat, part, pstat, out_weight, wsib)


def solution(mesh):
    return jax.shard_map(
        shards,
        mesh=mesh,
        in_specs=(
            P("ctx", "mp"),
            P("ctx", "mp"),
            P("ctx", "mp"),
            P("mp", None),
            P("ctx", None),
            P(),
        ),
        out_specs=P(("ctx", "mp"), None),
        check_vma=False,
    )
```

```python
import math

import jax
import jax.numpy as jnp
from jax import lax
from jax.experimental import pallas as pl
from jax.experimental.pallas import tpu as pltpu
from jax.sharding import PartitionSpec as P

HD = 128
BLK = 128
RAND = 3
GLOB = 2
CAND = GLOB + RAND
NZ = 8
NY = 4
NX = 4
HEADS = 4
PAIR = 2 * HD
QB = 4
FEATS = HEADS * HD
WIDTH = 4096
HALF = BLK // 2
TILE = 512
SCALE = 1.0 / math.sqrt(HD)
LOW = -1e30
MESH = pl.DeviceIdType.MESH
NT = (((1,), (1,)), ((), ()))
RING = 28
MIB = 1024 * 1024


def kernel(
    q_ref, k_ref, v_ref, w_ref, ids_ref, glob_ref, out_ref,
    k_col, v_col0, v_col1, q_row, id_row, id_s, k_ext, v_ext, v_own, acc, w_stat,
    probs, part, p_stat, got, got_stat, w_own, w_other, att, att_other, sent, relay, final, total,
    ring_send, ring_recv, row_send, row_recv, edge_send, edge_recv, w_sem, local_sem,
    part_send, part_recv, stat_send, stat_recv, att_send, att_recv, x_send, x_recv,
):
    me, mp = lax.axis_index("ctx"), lax.axis_index("mp")
    z, y, x, core = me // NY, me % NY, mp // 2, mp % 2
    count = NZ * NY
    after, before = (me + 1) % count, (me + count - 1) % count
    sibling = mp + 1 - 2 * core
    up, down = (z + 1) % NZ, (z + NZ - 1) % NZ
    right, left = ((x + 1) % NX) * 2 + core, ((x + NX - 1) % NX) * 2 + core
    order = [(x + d) % NX for d in (2, 1, 3, 0)]
    v_cols = (v_col0, v_col1)

    local = [
        pltpu.make_async_copy(v_ref, v_own, local_sem.at[0]),
        pltpu.make_async_copy(q_ref, q_row.at[pl.ds(y * QB, QB)], local_sem.at[1]),
        pltpu.make_async_copy(k_ref, k_ext.at[pl.ds(1, QB)], local_sem.at[2]),
        pltpu.make_async_copy(k_ref, k_col.at[pl.ds(z * QB, QB)], local_sem.at[3]),
        pltpu.make_async_copy(ids_ref, id_row.at[y], local_sem.at[4]),
        pltpu.make_async_copy(w_ref, w_own, local_sem.at[5]),
    ]
    for copy in local:
        copy.start()

    barrier = pltpu.get_barrier_semaphore()
    peers = [{"ctx": up * NY + y}, {"ctx": down * NY + y}]
    peers += [{"ctx": z * NY + (y + d) % NY} for d in range(1, NY)]
    peers += [{"ctx": after}, {"ctx": before}, {"mp": sibling}, {"mp": right}, {"mp": left}]
    for peer in peers:
        pl.semaphore_signal(barrier, inc=1, device_id=peer, device_id_type=MESH)
    pl.semaphore_wait(barrier, len(peers))

    def remote(src, dst, send, recv, peer):
        return pltpu.make_async_remote_copy(
            src_ref=src, dst_ref=dst, send_sem=send, recv_sem=recv, device_id=peer, device_id_type=MESH
        )

    def ring(way, i):
        sign = 1 if way == 0 else -1
        peer = {"ctx": (up if way == 0 else down) * NY + y}
        sems = (ring_send.at[way, i], ring_recv.at[way, i])
        if i < 14:
            back, piece = i // 4, (i % 4 + 2 * way) % 4
            first = ((z + NZ - sign * back) % NZ) * QB
            src = k_ref.at[piece] if back == 0 else k_col.at[first + piece]
            return remote(src, k_col.at[first + piece], *sems, peer)
        heads, j = (i - 14) // 7, (i - 14) % 7
        back, piece = j // 2, (j % 2 + way) % 2
        first = ((z + NZ - sign * back) % NZ) * QB
        span = v_cols[heads].at[pl.ds(first + 2 * piece, 2)]
        return remote(span, span, *sems, peer)

    rings = [[ring(way, i) for i in range(RING)] for way in range(2)]
    follow = {r: [r + 4] for r in range(10)}
    follow[9] += [14, 15]
    for start in (14, 21):
        for r in range(start, start + 5):
            follow[r] = [r + 2]
    follow[18] += [21, 22]

    def advance(r):
        for way in range(2):
            rings[way][r].wait_recv()
            for s in follow.get(r, ()):
                rings[way][s].start()

    for i in range(4):
        rings[0][i].start()
        rings[1][i].start()
    edges = [
        remote(k_ref.at[QB - 1], k_ext.at[0], edge_send.at[0], edge_recv.at[0], {"ctx": after}),
        remote(k_ref.at[0], k_ext.at[QB + 1], edge_send.at[1], edge_recv.at[1], {"ctx": before}),
        remote(v_ext.at[QB], v_ext.at[0], edge_send.at[2], edge_recv.at[2], {"ctx": after}),
        remote(v_ext.at[1], v_ext.at[QB + 1], edge_send.at[3], edge_recv.at[3], {"ctx": before}),
    ]
    edges[0].start()
    edges[1].start()
    rows = []
    for d in range(1, NY):
        peer = {"ctx": z * NY + (y + d) % NY}
        rows.append(remote(ids_ref, id_row.at[y], row_send.at[1, d - 1], row_recv.at[1, d - 1], peer))
        rows.append(remote(q_ref, q_row.at[pl.ds(y * QB, QB)], row_send.at[0, d - 1], row_recv.at[0, d - 1], peer))
    for copy in rows:
        copy.start()
    weight = remote(w_ref, w_other, w_sem.at[0], w_sem.at[1], {"mp": sibling})
    weight.start()

    local[0].wait()

    def turn(b, carry):
        for h in range(HEADS):
            flipped = v_own[b, :, pl.ds(h * HD, HD)].T
            v_ext[b + 1, pl.ds(h * HD, HD), :] = flipped
            v_cols[h // 2][z * QB + b, pl.ds((h % 2) * HD, HD), :] = flipped
        return carry

    lax.fori_loop(0, QB, turn, 0)
    edges[2].start()
    edges[3].start()
    advance(0)
    for copy in local[1:]:
        copy.wait()
    for copy in edges:
        copy.wait_recv()

    def window(qb):
        row = lax.broadcasted_iota(jnp.int32, (3 * BLK, 1), 0)
        first = jnp.where(me + qb == 0, BLK, 0)
        last = jnp.where(me * QB + qb == count * QB - 1, 2 * BLK, 3 * BLK)
        live = (row >= first) & (row < last)
        for h in range(HEADS):
            cols = pl.ds(h * HD, HD)
            keys = jnp.concatenate([k_ext[qb + j, :, cols] for j in range(3)], axis=0)
            values = jnp.concatenate([v_ext[qb + j, cols, :] for j in range(3)], axis=1)
            s = lax.dot_general(keys, q_row[y * QB + qb, :, cols], NT, preferred_element_type=jnp.float32) * SCALE
            s = jnp.where(live, s, LOW)
            top = jnp.max(s, axis=0, keepdims=True)
            p = jnp.exp(s - top).astype(jnp.bfloat16)
            w_stat[qb, pl.ds(h, 1), :] = top
            w_stat[qb, pl.ds(HEADS + h, 1), :] = jnp.sum(p.astype(jnp.float32), axis=0, keepdims=True)
            acc[qb, cols, :] = jnp.dot(values, p, preferred_element_type=jnp.float32)

    for r in range(1, 10):
        if r <= QB:
            window(r - 1)
        advance(r)

    for copy in rows:
        copy.wait_recv()
    to_scalar = pltpu.make_async_copy(id_row, id_s, local_sem.at[6])
    to_scalar.start()
    to_scalar.wait()
    for r in range(10, 14):
        advance(r)

    def candidates(t):
        blocks = [glob_ref[j] for j in range(GLOB)]
        blocks += [id_s[lax.div(t, QB), lax.rem(t, QB), j] for j in range(RAND)]
        spots = [lax.div(block, NY * QB) * QB + lax.rem(block, QB) for block in blocks]
        return blocks, spots

    def score(t, carry):
        blocks, spots = candidates(t)
        bias = [jnp.where(lax.rem(lax.div(block, QB), NY) == y, 0.0, LOW) for block in blocks]
        for h in range(HEADS):
            cols = pl.ds(h * HD, HD)
            keys = jnp.concatenate([k_col[spot, :, cols] for spot in spots], axis=0)
            s = lax.dot_general(keys, q_row[t, :, cols], NT, preferred_element_type=jnp.float32)
            s = jnp.concatenate([s[j * BLK:(j + 1) * BLK] * SCALE + bias[j] for j in range(CAND)], axis=0)
            top = jnp.max(s, axis=0, keepdims=True)
            p = jnp.exp(s - top).astype(jnp.bfloat16)
            p_stat[t, pl.ds(h, 1), :] = top
            p_stat[t, pl.ds(HEADS + h, 1), :] = jnp.sum(p.astype(jnp.float32), axis=0, keepdims=True)
            probs[t, h] = p
        return carry

    steps = [0, 3, 6, 9, 12, 14, 16]
    for n, r in enumerate(range(14, 20)):
        lax.fori_loop(steps[n], steps[n + 1], score, 0)
        advance(r)

    stats = []
    for d in range(1, NY):
        to = (y + d) % NY
        stats.append(remote(p_stat.at[pl.ds(to * QB, QB)], got_stat.at[d - 1], stat_send.at[d - 1],
                            stat_recv.at[d - 1], {"ctx": z * NY + to}))
        stats[-1].start()
    advance(20)

    def returns(pair, i):
        qb = order[i]
        span = pl.ds(pair * PAIR, PAIR)
        copies = []
        for d in (2, 1, 3):
            to = (y + d) % NY
            copies.append(remote(part.at[to * QB + qb, span], got.at[d - 1, qb, span],
                                 part_send.at[pair, d - 1, i], part_recv.at[pair, d - 1, i], {"ctx": z * NY + to}))
        return copies

    def weigh(pair, i):
        qb = order[i]

        def one(to, carry):
            t = to * QB + qb
            spots = candidates(t)[1]
            for g in range(2):
                h = 2 * pair + g
                values = jnp.concatenate([v_cols[pair][spot, pl.ds(g * HD, HD), :] for spot in spots], axis=1)
                out = jnp.dot(values, probs[t, h], preferred_element_type=jnp.float32)
                out = out / p_stat[t, pl.ds(HEADS + h, 1), :]
                part[t, pl.ds(h * HD, HD), :] = out.astype(jnp.bfloat16)
            return carry

        lax.fori_loop(0, NY, one, 0)

    def merge(pair, i):
        qb = order[i]
        for g in range(2):
            h = 2 * pair + g
            cols = pl.ds(h * HD, HD)
            line, low_line = pl.ds(h, 1), pl.ds(HEADS + h, 1)
            tops = [w_stat[qb, line, :], p_stat[y * QB + qb, line, :]]
            tops += [got_stat[s, qb, line, :] for s in range(NY - 1)]
            sums = [w_stat[qb, low_line, :], p_stat[y * QB + qb, low_line, :]]
            sums += [got_stat[s, qb, low_line, :] for s in range(NY - 1)]
            best = tops[0]
            for top in tops[1:]:
                best = jnp.maximum(best, top)
            scales = [jnp.exp(top - best) for top in tops]
            weights = [scale * total_of for scale, total_of in zip(scales, sums)]
            low = weights[0] + weights[1] + weights[2] + weights[3] + weights[4]
            value = acc[qb, cols, :] * (scales[0] / low)
            value += part[y * QB + qb, cols, :].astype(jnp.float32) * (weights[1] / low)
            for s in range(NY - 1):
                value += got[s, qb, cols, :].astype(jnp.float32) * (weights[s + 2] / low)
            att[i, :, cols] = value.T.astype(jnp.bfloat16)

    parts = [[returns(pair, i) for i in range(QB)] for pair in range(2)]
    for i in range(QB):
        weigh(0, i)
        for copy in parts[0][i]:
            copy.start()
        advance(21 + i)
    for copy in stats:
        copy.wait_recv()
    weight.wait()
    for n, r in enumerate((25, 26)):
        for i in (2 * n, 2 * n + 1):
            for copy in parts[0][i]:
                copy.wait_recv()
            merge(0, i)
        advance(r)
    advance(27)

    for i in range(QB):
        weigh(1, i)
        for copy in parts[1][i]:
            copy.start()

    swaps, sends = [], []
    mine = pl.ds(pl.multiple_of(core * HALF, HALF), HALF)
    theirs = pl.ds(pl.multiple_of((1 - core) * HALF, HALF), HALF)
    middle = WIDTH // 2
    for i in range(QB):
        for copy in parts[1][i]:
            copy.wait_recv()
        merge(1, i)
        swaps.append(remote(att.at[i, theirs], att_other.at[i], att_send.at[i], att_recv.at[i], {"mp": sibling}))
        swaps[i].start()

        def own(n, carry):
            cols = pl.ds(pl.multiple_of(n * TILE, TILE), TILE)
            total[:, cols] = jnp.dot(att[i, mine, :], w_own[:, cols], preferred_element_type=jnp.float32)
            return carry

        lax.fori_loop(0, WIDTH // TILE, own, 0)
        swaps[i].wait_recv()
        if 1 <= i < 3:
            sends[i - 1].wait_recv()
        if i == 3:
            sends[2].wait_recv()
            sends[3].wait_recv()

        def other(n, carry):
            cols = pl.ds(pl.multiple_of(n * TILE, TILE), TILE)
            value = total[:, cols] + jnp.dot(att_other[i], w_other[:, cols], preferred_element_type=jnp.float32)
            if i == 3:
                value += final[0, :, cols].astype(jnp.float32) + final[1, :, cols].astype(jnp.float32)
                out_ref[:, cols] = value.astype(jnp.bfloat16)
            else:
                sent[i, :, cols] = value.astype(jnp.bfloat16)
            return carry

        def other_relay(n, carry):
            place = n * TILE + (i - 1) * middle
            cols = pl.ds(pl.multiple_of(place, TILE), TILE)
            near = pl.ds(pl.multiple_of(n * TILE, TILE), TILE)
            value = total[:, cols] + jnp.dot(att_other[i], w_other[:, cols], preferred_element_type=jnp.float32)
            sent[i, :, cols] = (value + relay[i - 1, :, near].astype(jnp.float32)).astype(jnp.bfloat16)
            return carry

        tiles = WIDTH // TILE
        if i == 1:
            lax.fori_loop(tiles // 2, tiles, other, 0)
            lax.fori_loop(0, tiles // 2, other_relay, 0)
        elif i == 2:
            lax.fori_loop(0, tiles // 2, other, 0)
            lax.fori_loop(0, tiles // 2, other_relay, 0)
        else:
            lax.fori_loop(0, tiles, other, 0)
        if i == 0:
            for s, peer in enumerate((right, left)):
                sends.append(remote(sent.at[0, :, pl.ds(s * middle, middle)], relay.at[s],
                                    x_send.at[s], x_recv.at[s], {"mp": peer}))
                sends[-1].start()
        elif i < 3:
            sends.append(remote(sent.at[i], final.at[i - 1], x_send.at[i + 1], x_recv.at[i + 1],
                                {"mp": right if i == 1 else left}))
            sends[-1].start()

    for copy in edges + rings[0] + rings[1] + rows + stats + swaps + sends:
        copy.wait_send()
    for copies in parts[0] + parts[1]:
        for copy in copies:
            copy.wait_send()


def shards(query_rows, key_rows, value_rows, out_weight, random_ids, global_ids):
    bf, f32 = jnp.bfloat16, jnp.float32
    dma = pltpu.SemaphoreType.DMA
    vmem = pltpu.VMEM
    ids = jnp.pad(random_ids, ((0, 8 - QB), (0, 128 - RAND)))
    anywhere = pl.BlockSpec(memory_space=pl.ANY)
    blocks = (QB, BLK, FEATS)
    return pl.pallas_call(
        kernel,
        name="attend_and_project",
        out_shape=jax.ShapeDtypeStruct((HALF, WIDTH), bf),
        in_specs=[anywhere] * 5 + [pl.BlockSpec(memory_space=pltpu.SMEM)],
        out_specs=pl.BlockSpec(memory_space=pltpu.VMEM),
        scratch_shapes=[
            vmem((NZ * QB, BLK, FEATS), bf),
            vmem((NZ * QB, PAIR, BLK), bf),
            vmem((NZ * QB, PAIR, BLK), bf),
            vmem((NY * QB, BLK, FEATS), bf),
            vmem((NY, 8, 128), jnp.int32),
            pltpu.SMEM((NY, 8, 128), jnp.int32),
            vmem((QB + 2, BLK, FEATS), bf),
            vmem((QB + 2, FEATS, BLK), bf),
            vmem(blocks, bf),
            vmem((QB, FEATS, BLK), f32),
            vmem((QB, 2 * HEADS, BLK), f32),
            vmem((NY * QB, HEADS, CAND * BLK, BLK), bf),
            vmem((NY * QB, FEATS, BLK), bf),
            vmem((NY * QB, 2 * HEADS, BLK), f32),
            vmem((NY - 1, QB, FEATS, BLK), bf),
            vmem((NY - 1, QB, 2 * HEADS, BLK), f32),
            vmem((FEATS, WIDTH), bf),
            vmem((FEATS, WIDTH), bf),
            vmem((QB, BLK, FEATS), bf),
            vmem((QB, HALF, FEATS), bf),
            vmem((3, HALF, WIDTH), bf),
            vmem((2, HALF, WIDTH // 2), bf),
            vmem((2, HALF, WIDTH), bf),
            vmem((HALF, WIDTH), f32),
            dma((2, RING)), dma((2, RING)), dma((2, NY - 1)), dma((2, NY - 1)),
            dma((4,)), dma((4,)), dma((2,)), dma((7,)),
            dma((2, NY - 1, QB)), dma((2, NY - 1, QB)), dma((NY - 1,)), dma((NY - 1,)),
            dma((QB,)), dma((QB,)), dma((4,)), dma((4,)),
        ],
        compiler_params=pltpu.CompilerParams(
            collective_id=0, has_side_effects=True, vmem_limit_bytes=56 * MIB
        ),
        cost_estimate=pl.CostEstimate(flops=4 * 10**9, bytes_accessed=24 * MIB, transcendentals=0),
    )(
        query_rows.reshape(blocks), key_rows.reshape(blocks), value_rows.reshape(blocks),
        out_weight, ids, global_ids,
    )


def solution(mesh):
    return jax.shard_map(
        shards,
        mesh=mesh,
        in_specs=(
            P("ctx", "mp"),
            P("ctx", "mp"),
            P("ctx", "mp"),
            P("mp", None),
            P("ctx", None),
            P(),
        ),
        out_specs=P(("ctx", "mp"), None),
        check_vma=False,
    )
```

```python
import math

import jax
import jax.numpy as jnp
from jax import lax
from jax.experimental import pallas as pl
from jax.experimental.pallas import tpu as pltpu
from jax.sharding import PartitionSpec as P

HD = 128
BLK = 128
RAND = 3
GLOB = 2
CAND = GLOB + RAND
NZ = 8
NY = 4
NX = 4
HEADS = 4
QB = 4
FEATS = HEADS * HD
WIDTH = 4096
HALF = BLK // 2
TILE = 512
SCALE = 1.0 / math.sqrt(HD)
LOW = -1e30
MESH = pl.DeviceIdType.MESH
NT = (((1,), (1,)), ((), ()))
PHASES = 1 + HEADS
TILES = WIDTH // TILE
MIDDLE = WIDTH // 2
MIB = 1024 * 1024


def ring_order():
    order = [(0, 0, j) for j in range(4)]
    for p in range(PHASES):
        ahead = [(p + 1, 0, j) for j in range(4)] if p + 1 < PHASES else []
        order += [(p, 1, j) for j in range(4)] + ahead[:2]
        order += [(p, 2, j) for j in range(4)] + ahead[2:]
        order += [(p, 3, j) for j in range(2)]
    return order


ORDER = ring_order()
RING = len(ORDER)
SPOT = {item: n for n, item in enumerate(ORDER)}
DONE = [SPOT[p, 3, 1] for p in range(PHASES)]


def followers():
    follow, last = {}, -1
    for n, (p, back, j) in enumerate(ORDER):
        if back > 0:
            last = max(last, SPOT[p, back - 1, j])
        follow.setdefault(last, []).append(n)
    return follow


def kernel(
    q_ref, k_ref, v_ref, w_ref, ids_ref, glob_ref, out_ref,
    k_col, v_col0, v_col1, v_col2, v_col3, q_row, id_row, id_s, k_edge, v_edge, v_own, acc, w_stat, w_probs,
    probs, part, p_stat, got, got_stat, w_own, w_other, att, att_other, sent, relay, final, total,
    ring_send, ring_recv, row_send, row_recv, id_send, id_recv, edge_send, edge_recv, w_sem, local_sem,
    part_send, part_recv, stat_send, stat_recv, att_send, att_recv, x_send, x_recv,
):
    me, mp = lax.axis_index("ctx"), lax.axis_index("mp")
    z, y, x, core = me // NY, me % NY, mp // 2, mp % 2
    count = NZ * NY
    sibling = mp + 1 - 2 * core
    up, down = (z + 1) % NZ, (z + NZ - 1) % NZ
    right, left = ((x + 1) % NX) * 2 + core, ((x + NX - 1) % NX) * 2 + core
    order = [(x + d) % NX for d in (2, 1, 3, 0)]
    v_cols = (v_col0, v_col1, v_col2, v_col3)

    local = [
        pltpu.make_async_copy(v_ref, v_own, local_sem.at[0]),
        pltpu.make_async_copy(q_ref, q_row.at[pl.ds(y * QB, QB)], local_sem.at[1]),
        pltpu.make_async_copy(k_ref, k_col.at[pl.ds(z * QB, QB)], local_sem.at[2]),
        pltpu.make_async_copy(ids_ref, id_row.at[y], local_sem.at[3]),
        pltpu.make_async_copy(w_ref, w_own, local_sem.at[4]),
    ]
    for copy in local:
        copy.start()

    barrier = pltpu.get_barrier_semaphore()
    peers = [{"ctx": up * NY + y}, {"ctx": down * NY + y}]
    peers += [{"ctx": z * NY + (y + d) % NY} for d in range(1, NY)]
    peers += [{"mp": sibling}, {"mp": right}, {"mp": left}]
    for peer in peers:
        pl.semaphore_signal(barrier, inc=1, device_id=peer, device_id_type=MESH)
    pl.semaphore_wait(barrier, len(peers))

    def remote(src, dst, send, recv, peer):
        return pltpu.make_async_remote_copy(
            src_ref=src, dst_ref=dst, send_sem=send, recv_sem=recv, device_id=peer, device_id_type=MESH
        )

    def ring(way, n):
        p, back, j = ORDER[n]
        sign = 1 if way == 0 else -1
        peer = {"ctx": (up if way == 0 else down) * NY + y}
        sems = (ring_send.at[way, n], ring_recv.at[way, n])
        piece = (j + 2 * way) % 4
        block = ((z + NZ - sign * back) % NZ) * QB + piece
        if p > 0:
            return remote(v_cols[p - 1].at[block], v_cols[p - 1].at[block], *sems, peer)
        return remote(k_ref.at[piece] if back == 0 else k_col.at[block], k_col.at[block], *sems, peer)

    rings = [[ring(way, n) for n in range(RING)] for way in range(2)]
    follow = followers()
    for n in follow[-1]:
        rings[0][n].start()
        rings[1][n].start()

    above = jnp.where(y < NY - 1, z, down) * QB + QB - 1
    below = jnp.where(y > 0, z, up) * QB
    next_y, last_y = {"ctx": z * NY + (y + 1) % NY}, {"ctx": z * NY + (y + NY - 1) % NY}
    edges = []
    for p in range(PHASES):
        source = k_col if p == 0 else v_cols[p - 1]
        target = k_edge if p == 0 else v_edge
        spots = (0, 1) if p == 0 else (2 * p - 2, 2 * p - 1)
        edges.append([
            remote(source.at[above], target.at[spots[0]], edge_send.at[p, 0], edge_recv.at[p, 0], next_y),
            remote(source.at[below], target.at[spots[1]], edge_send.at[p, 1], edge_recv.at[p, 1], last_y),
        ])
    numbers, rows = [], []
    for d in range(1, NY):
        peer = {"ctx": z * NY + (y + d) % NY}
        numbers.append(remote(ids_ref, id_row.at[y], id_send.at[d - 1], id_recv.at[d - 1], peer))
        for b in range(QB):
            rows.append(remote(q_ref.at[b], q_row.at[y * QB + b], row_send.at[d - 1, b], row_recv.at[d - 1, b], peer))
    for copy in numbers:
        copy.start()
    weight = remote(w_ref, w_other, w_sem.at[0], w_sem.at[1], {"mp": sibling})
    weight.start()

    local[0].wait()

    def turn(b, carry):
        for h in range(HEADS):
            v_cols[h][z * QB + b] = v_own[b, :, pl.ds(h * HD, HD)].T
        return carry

    lax.fori_loop(0, QB, turn, 0)
    for copy in local[1:]:
        copy.wait()

    def window_score(qb):
        row = lax.broadcasted_iota(jnp.int32, (3 * BLK, 1), 0)
        first = jnp.where(me + qb == 0, BLK, 0)
        last = jnp.where(me * QB + qb == count * QB - 1, 2 * BLK, 3 * BLK)
        live = (row >= first) & (row < last)
        for h in range(HEADS):
            cols = pl.ds(h * HD, HD)
            keys = [k_edge[0, :, cols] if qb == 0 else k_col[z * QB + qb - 1, :, cols]]
            keys.append(k_col[z * QB + qb, :, cols])
            keys.append(k_edge[1, :, cols] if qb == QB - 1 else k_col[z * QB + qb + 1, :, cols])
            s = lax.dot_general(jnp.concatenate(keys, axis=0), q_row[y * QB + qb, :, cols], NT,
                                preferred_element_type=jnp.float32) * SCALE
            s = jnp.where(live, s, LOW)
            top = jnp.max(s, axis=0, keepdims=True)
            p = jnp.exp(s - top).astype(jnp.bfloat16)
            w_stat[qb, pl.ds(h, 1), :] = top
            w_stat[qb, pl.ds(HEADS + h, 1), :] = jnp.sum(p.astype(jnp.float32), axis=0, keepdims=True)
            w_probs[qb, h] = p

    def window_weigh(h):
        for copy in edges[h + 1]:
            copy.wait_recv()
        for qb in range(QB):
            values = [v_edge[2 * h] if qb == 0 else v_cols[h][z * QB + qb - 1]]
            values.append(v_cols[h][z * QB + qb])
            values.append(v_edge[2 * h + 1] if qb == QB - 1 else v_cols[h][z * QB + qb + 1])
            acc[qb, pl.ds(h * HD, HD), :] = jnp.dot(
                jnp.concatenate(values, axis=1), w_probs[qb, h], preferred_element_type=jnp.float32)

    def candidates(t):
        blocks = [glob_ref[j] for j in range(GLOB)]
        blocks += [id_s[lax.div(t, QB), lax.rem(t, QB), j] for j in range(RAND)]
        spots = [lax.div(block, NY * QB) * QB + lax.rem(block, QB) for block in blocks]
        return blocks, spots

    def score(t, carry):
        blocks, spots = candidates(t)
        bias = [jnp.where(lax.rem(lax.div(block, QB), NY) == y, 0.0, LOW) for block in blocks]
        for h in range(HEADS):
            cols = pl.ds(h * HD, HD)
            keys = jnp.concatenate([k_col[spot, :, cols] for spot in spots], axis=0)
            s = lax.dot_general(keys, q_row[t, :, cols], NT, preferred_element_type=jnp.float32)
            s = jnp.concatenate([s[j * BLK:(j + 1) * BLK] * SCALE + bias[j] for j in range(CAND)], axis=0)
            top = jnp.max(s, axis=0, keepdims=True)
            p = jnp.exp(s - top).astype(jnp.bfloat16)
            p_stat[t, pl.ds(h, 1), :] = top
            p_stat[t, pl.ds(HEADS + h, 1), :] = jnp.sum(p.astype(jnp.float32), axis=0, keepdims=True)
            probs[t, h] = p
        return carry

    stats = []
    for d in range(1, NY):
        to = (y + d) % NY
        stats.append(remote(p_stat.at[pl.ds(to * QB, QB)], got_stat.at[d - 1], stat_send.at[d - 1],
                            stat_recv.at[d - 1], {"ctx": z * NY + to}))

    def returns(h, i):
        span = pl.ds(h * HD, HD)
        copies = []
        for d in (2, 1, 3):
            to = (y + d) % NY
            copies.append(remote(part.at[to * QB + order[i], span], got.at[d - 1, order[i], span],
                                 part_send.at[h, d - 1, i], part_recv.at[h, d - 1, i], {"ctx": z * NY + to}))
        return copies

    parts = [[returns(h, i) for i in range(QB)] for h in range(HEADS)]

    def weigh(h, i):
        def one(to, carry):
            t = to * QB + order[i]
            spots = candidates(t)[1]
            values = jnp.concatenate([v_cols[h][spot] for spot in spots], axis=1)
            out = jnp.dot(values, probs[t, h], preferred_element_type=jnp.float32)
            out = out / p_stat[t, pl.ds(HEADS + h, 1), :]
            part[t, pl.ds(h * HD, HD), :] = out.astype(jnp.bfloat16)
            return carry

        lax.fori_loop(0, NY, one, 0)
        for copy in parts[h][i]:
            copy.start()

    def merge(h, i):
        for copy in parts[h][i]:
            copy.wait_recv()
        qb = order[i]
        cols = pl.ds(h * HD, HD)
        line, low_line = pl.ds(h, 1), pl.ds(HEADS + h, 1)
        tops = [w_stat[qb, line, :], p_stat[y * QB + qb, line, :]]
        tops += [got_stat[s, qb, line, :] for s in range(NY - 1)]
        sums = [w_stat[qb, low_line, :], p_stat[y * QB + qb, low_line, :]]
        sums += [got_stat[s, qb, low_line, :] for s in range(NY - 1)]
        best = tops[0]
        for top in tops[1:]:
            best = jnp.maximum(best, top)
        scales = [jnp.exp(top - best) for top in tops]
        weights = [scale * total_of for scale, total_of in zip(scales, sums)]
        low = weights[0] + weights[1] + weights[2] + weights[3] + weights[4]
        value = acc[qb, cols, :] * (scales[0] / low)
        value += part[y * QB + qb, cols, :].astype(jnp.float32) * (weights[1] / low)
        for s in range(NY - 1):
            value += got[s, qb, cols, :].astype(jnp.float32) * (weights[s + 2] / low)
        att[i, :, cols] = value.T.astype(jnp.bfloat16)

    mine = pl.ds(pl.multiple_of(core * HALF, HALF), HALF)
    theirs = pl.ds(pl.multiple_of((1 - core) * HALF, HALF), HALF)
    early, late = pl.ds(0, 2 * HD), pl.ds(2 * HD, 2 * HD)
    swaps = [[remote(att.at[i, theirs, cols], att_other.at[i, :, cols], att_send.at[n, i], att_recv.at[n, i],
                     {"mp": sibling}) for i in range(QB)] for n, cols in enumerate((early, late))]

    def project_early(n, carry):
        cols = pl.ds(pl.multiple_of(n * TILE, TILE), TILE)
        own = jnp.concatenate([att[i, mine, early] for i in range(QB)], axis=0)
        other = jnp.concatenate([att_other[i, :, early] for i in range(QB)], axis=0)
        value = jnp.dot(own, w_own[early, cols], preferred_element_type=jnp.float32)
        value += jnp.dot(other, w_other[early, cols], preferred_element_type=jnp.float32)
        for i in range(QB):
            total[i, :, cols] = value[i * HALF:(i + 1) * HALF]
        return carry

    work = {}

    def at(r, *calls):
        work.setdefault(r, []).extend(calls)

    def edges_go(p):
        for copy in edges[p]:
            copy.start()

    def edges_come():
        for copy in edges[0]:
            copy.wait_recv()

    def rows_come():
        for copy in rows + numbers:
            copy.wait_recv()
        to_scalar = pltpu.make_async_copy(id_row, id_s, local_sem.at[5])
        to_scalar.start()
        to_scalar.wait()

    def stats_go():
        for copy in stats:
            copy.start()

    def stats_come():
        for copy in stats:
            copy.wait_recv()

    def swaps_go():
        for copy in swaps[0]:
            copy.start()

    def swaps_come():
        for copy in swaps[0]:
            copy.wait_recv()
        weight.wait()

    for n, b in enumerate([d * QB + b for b in range(QB) for d in range(NY - 1)]):
        at(n, rows[b].start)
    for p in range(PHASES):
        at(SPOT[p, 0, 3], lambda p=p: edges_go(p))
    at(6, edges_come)
    for qb in range(QB):
        at(6 + qb, lambda qb=qb: window_score(qb))
    at(DONE[0], rows_come)
    bounds = [0, 2, 4, 6, 8, 10, 12, 14, 16]
    for n in range(8):
        at(DONE[0] + n, lambda n=n: lax.fori_loop(bounds[n], bounds[n + 1], score, 0))
    at(DONE[0] + 8, stats_go)
    for h in range(HEADS - 1):
        for i in range(QB):
            at(DONE[h + 1] + i, lambda h=h, i=i: weigh(h, i))
        at(DONE[h + 1] + QB, lambda h=h: window_weigh(h))
    at(DONE[2] + 5, stats_come)
    for i in range(QB):
        at(DONE[2] + 6 + i, lambda i=i: merge(0, i))
        at(DONE[3] + 1 + i, lambda i=i: merge(1, i))
    at(DONE[3] + 5, swaps_go)
    at(DONE[3] + 7, swaps_come, lambda: lax.fori_loop(0, TILES // 2, project_early, 0))
    at(DONE[3] + 8, lambda: lax.fori_loop(TILES // 2, TILES, project_early, 0))
    assert max(work) < RING

    for r in range(RING):
        for way in range(2):
            rings[way][r].wait_recv()
            for n in follow.get(r, ()):
                rings[way][n].start()
        for call in work.get(r, ()):
            call()

    last = HEADS - 1
    for i in range(QB):
        weigh(last, i)
    window_weigh(last)

    sends = []
    for i in range(QB):
        merge(last - 1, i)
        merge(last, i)
        swaps[1][i].start()

        def own(n, carry):
            cols = pl.ds(pl.multiple_of(n * TILE, TILE), TILE)
            total[i, :, cols] += jnp.dot(att[i, mine, late], w_own[late, cols], preferred_element_type=jnp.float32)
            return carry

        lax.fori_loop(0, TILES, own, 0)
        swaps[1][i].wait_recv()
        if 1 <= i < 3:
            sends[i - 1].wait_recv()
        if i == 3:
            sends[2].wait_recv()
            sends[3].wait_recv()

        def value_of(cols):
            return total[i, :, cols] + jnp.dot(
                att_other[i, :, late], w_other[late, cols], preferred_element_type=jnp.float32)

        def other(n, carry):
            cols = pl.ds(pl.multiple_of(n * TILE, TILE), TILE)
            value = value_of(cols)
            if i == 3:
                value += final[0, :, cols].astype(jnp.float32) + final[1, :, cols].astype(jnp.float32)
                out_ref[:, cols] = value.astype(jnp.bfloat16)
            else:
                sent[i, :, cols] = value.astype(jnp.bfloat16)
            return carry

        def other_relay(n, carry):
            cols = pl.ds(pl.multiple_of(n * TILE + (i - 1) * MIDDLE, TILE), TILE)
            near = pl.ds(pl.multiple_of(n * TILE, TILE), TILE)
            value = value_of(cols) + relay[i - 1, :, near].astype(jnp.float32)
            sent[i, :, cols] = value.astype(jnp.bfloat16)
            return carry

        if i == 1:
            lax.fori_loop(TILES // 2, TILES, other, 0)
            lax.fori_loop(0, TILES // 2, other_relay, 0)
        elif i == 2:
            lax.fori_loop(0, TILES // 2, other, 0)
            lax.fori_loop(0, TILES // 2, other_relay, 0)
        else:
            lax.fori_loop(0, TILES, other, 0)
        if i == 0:
            for s, peer in enumerate((right, left)):
                sends.append(remote(sent.at[0, :, pl.ds(s * MIDDLE, MIDDLE)], relay.at[s],
                                    x_send.at[s], x_recv.at[s], {"mp": peer}))
                sends[-1].start()
        elif i < 3:
            sends.append(remote(sent.at[i], final.at[i - 1], x_send.at[i + 1], x_recv.at[i + 1],
                                {"mp": right if i == 1 else left}))
            sends[-1].start()

    groups = edges + rings + swaps + [rows, numbers, stats, sends] + [c for h in range(HEADS) for c in parts[h]]
    for copies in groups:
        for copy in copies:
            copy.wait_send()


def shards(query_rows, key_rows, value_rows, out_weight, random_ids, global_ids):
    bf, f32 = jnp.bfloat16, jnp.float32
    dma = pltpu.SemaphoreType.DMA
    vmem = pltpu.VMEM
    ids = jnp.pad(random_ids, ((0, 8 - QB), (0, 128 - RAND)))
    anywhere = pl.BlockSpec(memory_space=pl.ANY)
    blocks = (QB, BLK, FEATS)
    return pl.pallas_call(
        kernel,
        name="attend_and_project",
        out_shape=jax.ShapeDtypeStruct((HALF, WIDTH), bf),
        in_specs=[anywhere] * 5 + [pl.BlockSpec(memory_space=pltpu.SMEM)],
        out_specs=pl.BlockSpec(memory_space=pltpu.VMEM),
        scratch_shapes=[
            vmem((NZ * QB, BLK, FEATS), bf),
            *[vmem((NZ * QB, HD, BLK), bf)] * HEADS,
            vmem((NY * QB, BLK, FEATS), bf),
            vmem((NY, 8, 128), jnp.int32),
            pltpu.SMEM((NY, 8, 128), jnp.int32),
            vmem((2, BLK, FEATS), bf),
            vmem((2 * HEADS, HD, BLK), bf),
            vmem(blocks, bf),
            vmem((QB, FEATS, BLK), f32),
            vmem((QB, 2 * HEADS, BLK), f32),
            vmem((QB, HEADS, 3 * BLK, BLK), bf),
            vmem((NY * QB, HEADS, CAND * BLK, BLK), bf),
            vmem((NY * QB, FEATS, BLK), bf),
            vmem((NY * QB, 2 * HEADS, BLK), f32),
            vmem((NY - 1, QB, FEATS, BLK), bf),
            vmem((NY - 1, QB, 2 * HEADS, BLK), f32),
            vmem((FEATS, WIDTH), bf),
            vmem((FEATS, WIDTH), bf),
            vmem((QB, BLK, FEATS), bf),
            vmem((QB, HALF, FEATS), bf),
            vmem((3, HALF, WIDTH), bf),
            vmem((2, HALF, WIDTH // 2), bf),
            vmem((2, HALF, WIDTH), bf),
            vmem((QB, HALF, WIDTH), f32),
            dma((2, RING)), dma((2, RING)), dma((NY - 1, QB)), dma((NY - 1, QB)), dma((NY - 1,)), dma((NY - 1,)),
            dma((PHASES, 2)), dma((PHASES, 2)), dma((2,)), dma((6,)),
            dma((HEADS, NY - 1, QB)), dma((HEADS, NY - 1, QB)), dma((NY - 1,)), dma((NY - 1,)),
            dma((2, QB)), dma((2, QB)), dma((4,)), dma((4,)),
        ],
        compiler_params=pltpu.CompilerParams(
            collective_id=0, has_side_effects=True, vmem_limit_bytes=56 * MIB
        ),
        cost_estimate=pl.CostEstimate(flops=4 * 10**9, bytes_accessed=24 * MIB, transcendentals=0),
    )(
        query_rows.reshape(blocks), key_rows.reshape(blocks), value_rows.reshape(blocks),
        out_weight, ids, global_ids,
    )


def solution(mesh):
    return jax.shard_map(
        shards,
        mesh=mesh,
        in_specs=(
            P("ctx", "mp"),
            P("ctx", "mp"),
            P("ctx", "mp"),
            P("mp", None),
            P("ctx", None),
            P(),
        ),
        out_specs=P(("ctx", "mp"), None),
        check_vma=False,
    )
```

```python
import math

import jax
import jax.numpy as jnp
from jax import lax
from jax.experimental import pallas as pl
from jax.experimental.pallas import tpu as pltpu
from jax.sharding import PartitionSpec as P

HD = 128
BLK = 128
RAND = 3
GLOB = 2
CAND = GLOB + RAND
NZ = 8
NY = 4
NX = 4
HEADS = 4
QB = 4
FEATS = HEADS * HD
WIDTH = 4096
HALF = BLK // 2
TILE = 512
SCALE = 1.0 / math.sqrt(HD)
LOW = -1e30
MESH = pl.DeviceIdType.MESH
NT = (((1,), (1,)), ((), ()))
PHASES = 2 + HEADS
LATE = HEADS - 1
MAIN = LATE * HD
KINDS = ((0, 0), (1, 0), (1, 1), (1, 2), (0, 1), (1, 3))
V_PHASE = (1, 2, 3, 5)
CUTS = 4
CUT = HD // CUTS
TILES = WIDTH // TILE
MIDDLE = WIDTH // 2
MIB = 1024 * 1024


def ring_order():
    order = [(0, 0, j) for j in range(4)]
    for p in range(PHASES):
        ahead = [(p + 1, 0, j) for j in range(4)] if p + 1 < PHASES else []
        order += [(p, 1, j) for j in range(4)] + ahead[:2]
        order += [(p, 2, j) for j in range(4)] + ahead[2:]
        order += [(p, 3, j) for j in range(2)]
    return order


ORDER = ring_order()
RING = len(ORDER)
SPOT = {item: n for n, item in enumerate(ORDER)}
DONE = [SPOT[p, 3, 1] for p in range(PHASES)]


def followers():
    follow, last = {}, -1
    for n, (p, back, j) in enumerate(ORDER):
        if back > 0:
            last = max(last, SPOT[p, back - 1, j])
        follow.setdefault(last, []).append(n)
    return follow


def kernel(
    q_ref, k_ref, v_ref, w_ref, ids_ref, glob_ref, out_ref,
    k_main, k_late, v_col0, v_col1, v_col2, v_col3, q_row, id_row, id_s, k_edge, k_edge_late, v_edge, v_own, acc, w_stat, w_probs,
    probs, part, p_stat, p_late, got, got_stat, got_late, w_own, w_other, w_far,
    att, att_other, att_late, come_late, sent, relay, final, total,
    ring_send, ring_recv, row_send, row_recv, id_send, id_recv, edge_send, edge_recv, w_sem, local_sem,
    part_send, part_recv, stat_send, stat_recv, att_send, att_recv, x_send, x_recv,
    far_send, far_recv, pass_send, pass_recv, late_send, late_recv,
):
    me, mp = lax.axis_index("ctx"), lax.axis_index("mp")
    z, y, x, core = me // NY, me % NY, mp // 2, mp % 2
    count = NZ * NY
    sibling = mp + 1 - 2 * core
    up, down = (z + 1) % NZ, (z + NZ - 1) % NZ
    right, left = ((x + 1) % NX) * 2 + core, ((x + NX - 1) % NX) * 2 + core
    order = [(x + d) % NX for d in (2, 1, 3, 0)]
    v_cols = (v_col0, v_col1, v_col2, v_col3)
    k_cols, k_edges = (k_main, k_late), (k_edge, k_edge_late)
    main, late = pl.ds(0, MAIN), pl.ds(MAIN, HD)

    local = [
        pltpu.make_async_copy(v_ref, v_own, local_sem.at[0]),
        pltpu.make_async_copy(q_ref, q_row.at[pl.ds(y * QB, QB)], local_sem.at[1]),
        pltpu.make_async_copy(k_ref.at[:, :, main], k_main.at[pl.ds(z * QB, QB)], local_sem.at[2]),
        pltpu.make_async_copy(k_ref.at[:, :, late], k_late.at[pl.ds(z * QB, QB)], local_sem.at[6]),
        pltpu.make_async_copy(ids_ref, id_row.at[y], local_sem.at[3]),
        pltpu.make_async_copy(w_ref, w_own, local_sem.at[4]),
    ]
    for copy in local:
        copy.start()

    barrier = pltpu.get_barrier_semaphore()
    peers = [{"ctx": up * NY + y}, {"ctx": down * NY + y}]
    peers += [{"ctx": z * NY + (y + d) % NY} for d in range(1, NY)]
    peers += [{"mp": sibling}] + [{"mp": ((x + d) % NX) * 2 + c} for d in range(1, NX) for c in range(2)]
    for peer in peers:
        pl.semaphore_signal(barrier, inc=1, device_id=peer, device_id_type=MESH)
    pl.semaphore_wait(barrier, len(peers))

    def remote(src, dst, send, recv, peer):
        return pltpu.make_async_remote_copy(
            src_ref=src, dst_ref=dst, send_sem=send, recv_sem=recv, device_id=peer, device_id_type=MESH
        )

    def ring(way, n):
        p, back, j = ORDER[n]
        sign = 1 if way == 0 else -1
        peer = {"ctx": (up if way == 0 else down) * NY + y}
        sems = (ring_send.at[way, n], ring_recv.at[way, n])
        piece = (j + 2 * way) % 4
        block = ((z + NZ - sign * back) % NZ) * QB + piece
        kind, index = KINDS[p]
        ref = (k_cols, v_cols)[kind][index]
        src = ref.at[block]
        if kind == 0 and back == 0:
            src = k_ref.at[piece, :, (main, late)[index]]
        return remote(src, ref.at[block], *sems, peer)

    rings = [[ring(way, n) for n in range(RING)] for way in range(2)]
    follow = followers()
    for n in follow[-1]:
        rings[0][n].start()
        rings[1][n].start()

    above = jnp.where(y < NY - 1, z, down) * QB + QB - 1
    below = jnp.where(y > 0, z, up) * QB
    next_y, last_y = {"ctx": z * NY + (y + 1) % NY}, {"ctx": z * NY + (y + NY - 1) % NY}
    edges = []
    for p, (kind, index) in enumerate(KINDS):
        source = (k_cols, v_cols)[kind][index]
        target = v_edge if kind else k_edges[index]
        spots = (2 * index, 2 * index + 1) if kind else (0, 1)
        edges.append([
            remote(source.at[above], target.at[spots[0]], edge_send.at[p, 0], edge_recv.at[p, 0], next_y),
            remote(source.at[below], target.at[spots[1]], edge_send.at[p, 1], edge_recv.at[p, 1], last_y),
        ])
    numbers, rows = [], []
    for d in range(1, NY):
        peer = {"ctx": z * NY + (y + d) % NY}
        numbers.append(remote(ids_ref, id_row.at[y], id_send.at[d - 1], id_recv.at[d - 1], peer))
        for b in range(QB):
            rows.append(remote(q_ref.at[b], q_row.at[y * QB + b], row_send.at[d - 1, b], row_recv.at[d - 1, b], peer))
    for copy in numbers:
        copy.start()
    weight = remote(w_ref, w_other, w_sem.at[0], w_sem.at[1], {"mp": sibling})
    weight.start()

    local[0].wait()

    def turn(b, carry):
        for h in range(HEADS):
            v_cols[h][z * QB + b] = v_own[b, :, pl.ds(h * HD, HD)].T
        return carry

    lax.fori_loop(0, QB, turn, 0)
    for copy in local[1:]:
        copy.wait()

    def key_part(h):
        return (k_late, k_edge_late, pl.ds(0, HD)) if h == LATE else (k_main, k_edge, pl.ds(h * HD, HD))

    def window_score(qb, heads):
        row = lax.broadcasted_iota(jnp.int32, (3 * BLK, 1), 0)
        first = jnp.where(me + qb == 0, BLK, 0)
        last = jnp.where(me * QB + qb == count * QB - 1, 2 * BLK, 3 * BLK)
        live = (row >= first) & (row < last)
        for h in heads:
            k_col, edge, cols = key_part(h)
            keys = [edge[0, :, cols] if qb == 0 else k_col[z * QB + qb - 1, :, cols]]
            keys.append(k_col[z * QB + qb, :, cols])
            keys.append(edge[1, :, cols] if qb == QB - 1 else k_col[z * QB + qb + 1, :, cols])
            s = lax.dot_general(jnp.concatenate(keys, axis=0), q_row[y * QB + qb, :, pl.ds(h * HD, HD)], NT,
                                preferred_element_type=jnp.float32) * SCALE
            s = jnp.where(live, s, LOW)
            top = jnp.max(s, axis=0, keepdims=True)
            p = jnp.exp(s - top).astype(jnp.bfloat16)
            w_stat[qb, pl.ds(h, 1), :] = top
            w_stat[qb, pl.ds(HEADS + h, 1), :] = jnp.sum(p.astype(jnp.float32), axis=0, keepdims=True)
            w_probs[qb, h] = p

    def window_weigh(h):
        for copy in edges[V_PHASE[h]]:
            copy.wait_recv()
        for qb in range(QB):
            values = [v_edge[2 * h] if qb == 0 else v_cols[h][z * QB + qb - 1]]
            values.append(v_cols[h][z * QB + qb])
            values.append(v_edge[2 * h + 1] if qb == QB - 1 else v_cols[h][z * QB + qb + 1])
            acc[qb, pl.ds(h * HD, HD), :] = jnp.dot(
                jnp.concatenate(values, axis=1), w_probs[qb, h], preferred_element_type=jnp.float32)

    def candidates(t):
        blocks = [glob_ref[j] for j in range(GLOB)]
        blocks += [id_s[lax.div(t, QB), lax.rem(t, QB), j] for j in range(RAND)]
        spots = [lax.div(block, NY * QB) * QB + lax.rem(block, QB) for block in blocks]
        return blocks, spots

    def stat_lines(h):
        return (0, 1) if h == LATE else (h, HEADS + h)

    def score(t, heads):
        blocks, spots = candidates(t)
        bias = [jnp.where(lax.rem(lax.div(block, QB), NY) == y, 0.0, LOW) for block in blocks]
        for h in heads:
            k_col, _, cols = key_part(h)
            stat = p_late if h == LATE else p_stat
            top_line, sum_line = stat_lines(h)
            keys = jnp.concatenate([k_col[spot, :, cols] for spot in spots], axis=0)
            s = lax.dot_general(keys, q_row[t, :, pl.ds(h * HD, HD)], NT, preferred_element_type=jnp.float32)
            s = jnp.concatenate([s[j * BLK:(j + 1) * BLK] * SCALE + bias[j] for j in range(CAND)], axis=0)
            top = jnp.max(s, axis=0, keepdims=True)
            p = jnp.exp(s - top).astype(jnp.bfloat16)
            stat[t, pl.ds(top_line, 1), :] = top
            stat[t, pl.ds(sum_line, 1), :] = jnp.sum(p.astype(jnp.float32), axis=0, keepdims=True)
            probs[t, h] = p

    def score_main(t, carry):
        score(t, range(LATE))
        return carry

    def score_late(t, carry):
        score(t, (LATE,))
        return carry

    stats = [[], []]
    for d in range(1, NY):
        to = (y + d) % NY
        for n, (stat, got_one) in enumerate(((p_stat, got_stat), (p_late, got_late))):
            stats[n].append(remote(stat.at[pl.ds(to * QB, QB)], got_one.at[d - 1], stat_send.at[n, d - 1],
                                   stat_recv.at[n, d - 1], {"ctx": z * NY + to}))

    def returns(h, i):
        span = pl.ds(h * HD, HD)
        copies = []
        for d in (2, 1, 3):
            to = (y + d) % NY
            copies.append(remote(part.at[to * QB + order[i], span], got.at[d - 1, order[i], span],
                                 part_send.at[h, d - 1, i], part_recv.at[h, d - 1, i], {"ctx": z * NY + to}))
        return copies

    parts = [[returns(h, i) for i in range(QB)] for h in range(HEADS)]

    def weigh(h, i):
        def one(to, carry):
            t = to * QB + order[i]
            spots = candidates(t)[1]
            values = jnp.concatenate([v_cols[h][spot] for spot in spots], axis=1)
            out = jnp.dot(values, probs[t, h], preferred_element_type=jnp.float32)
            out = out / (p_late if h == LATE else p_stat)[t, pl.ds(stat_lines(h)[1], 1), :]
            part[t, pl.ds(h * HD, HD), :] = out.astype(jnp.bfloat16)
            return carry

        lax.fori_loop(0, NY, one, 0)
        for copy in parts[h][i]:
            copy.start()

    def merge(h, i):
        for copy in parts[h][i]:
            copy.wait_recv()
        qb = order[i]
        cols = pl.ds(h * HD, HD)
        line, low_line = pl.ds(h, 1), pl.ds(HEADS + h, 1)
        one, other = (p_late, got_late) if h == LATE else (p_stat, got_stat)
        there, low_there = [pl.ds(n, 1) for n in stat_lines(h)]
        tops = [w_stat[qb, line, :], one[y * QB + qb, there, :]]
        tops += [other[s, qb, there, :] for s in range(NY - 1)]
        sums = [w_stat[qb, low_line, :], one[y * QB + qb, low_there, :]]
        sums += [other[s, qb, low_there, :] for s in range(NY - 1)]
        best = tops[0]
        for top in tops[1:]:
            best = jnp.maximum(best, top)
        scales = [jnp.exp(top - best) for top in tops]
        weights = [scale * total_of for scale, total_of in zip(scales, sums)]
        low = weights[0] + weights[1] + weights[2] + weights[3] + weights[4]
        value = acc[qb, cols, :] * (scales[0] / low)
        value += part[y * QB + qb, cols, :].astype(jnp.float32) * (weights[1] / low)
        for s in range(NY - 1):
            value += got[s, qb, cols, :].astype(jnp.float32) * (weights[s + 2] / low)
        if h == LATE:
            att_late[i] = value.T.astype(jnp.bfloat16)
        else:
            att[i, :, cols] = value.T.astype(jnp.bfloat16)

    mine = pl.ds(pl.multiple_of(core * HALF, HALF), HALF)
    theirs = pl.ds(pl.multiple_of((1 - core) * HALF, HALF), HALF)
    swaps = [remote(att.at[i, theirs], att_other.at[i], att_send.at[i], att_recv.at[i], {"mp": sibling})
             for i in range(QB)]

    def project(n, carry):
        cols = pl.ds(pl.multiple_of(n * TILE, TILE), TILE)
        own = jnp.concatenate([att[i, mine, :] for i in range(QB)], axis=0)
        other = jnp.concatenate([att_other[i] for i in range(QB)], axis=0)
        value = jnp.dot(own, w_own[main, cols], preferred_element_type=jnp.float32)
        value += jnp.dot(other, w_other[main, cols], preferred_element_type=jnp.float32)
        for i in range(QB):
            total[i, :, cols] = value[i * HALF:(i + 1) * HALF]
        return carry

    far = [[], []]
    for way, peer in enumerate(({"mp": right}, {"mp": left})):
        from_d, to_d = (2, 0)[way], (2, 0)[way]
        for c in range(CUTS):
            rows_of = pl.ds(pl.multiple_of(core * HD + c * CUT, CUT), CUT)
            far[way].append(remote(w_ref.at[pl.ds(MAIN + c * CUT, CUT)], w_far.at[to_d, rows_of],
                                   far_send.at[way, c], far_recv.at[way, c], peer))
        for n in range(CUTS // 2):
            c = n + way * (CUTS // 2)
            rows_of = pl.ds(pl.multiple_of(core * HD + c * CUT, CUT), CUT)
            far[way].append(remote(w_far.at[from_d, rows_of], w_far.at[1, rows_of],
                                   far_send.at[way, CUTS + n], far_recv.at[way, CUTS + n], peer))
    own_half = pl.ds(pl.multiple_of(core * HD, HD), HD)
    passed = [remote(w_far.at[d, own_half], w_far.at[d, own_half], pass_send.at[d], pass_recv.at[d], {"mp": sibling})
              for d in range(NX - 1)]

    lates = []
    for i, qb in enumerate(order):
        lates.append([])
        for c in range(2):
            if i < QB - 1:
                lates[i].append(remote(att_late.at[i, pl.ds(c * HALF, HALF)], come_late.at[mp],
                                       late_send.at[i, c], late_recv.at[i, core], {"mp": qb * 2 + c}))
    lates[QB - 1].append(remote(att_late.at[QB - 1, theirs], come_late.at[mp],
                                late_send.at[QB - 1, 0], late_recv.at[QB - 1, core], {"mp": sibling}))

    sends = [remote(sent.at[0, :, pl.ds(s * MIDDLE, MIDDLE)], relay.at[s], x_send.at[s], x_recv.at[s], {"mp": peer})
             for s, peer in enumerate((right, left))]
    sends += [remote(sent.at[i], final.at[i - 1], x_send.at[i + 1], x_recv.at[i + 1], {"mp": peer})
              for i, peer in ((1, right), (2, left))]

    def send_first():
        sent[0] = total[0].astype(jnp.bfloat16)
        sends[0].start()
        sends[1].start()

    def send_relayed(i):
        sends[i - 1].wait_recv()
        here, there = pl.ds((i - 1) * MIDDLE, MIDDLE), pl.ds((2 - i) * MIDDLE, MIDDLE)
        sent[i, :, here] = (total[i, :, here] + relay[i - 1].astype(jnp.float32)).astype(jnp.bfloat16)
        sent[i, :, there] = total[i, :, there].astype(jnp.bfloat16)
        sends[i + 1].start()

    work = {}

    def at(r, *calls):
        work.setdefault(r, []).extend(calls)

    def edges_go(p):
        for copy in edges[p]:
            copy.start()

    def edges_come():
        for copy in edges[0]:
            copy.wait_recv()

    def rows_come():
        for copy in rows + numbers:
            copy.wait_recv()
        to_scalar = pltpu.make_async_copy(id_row, id_s, local_sem.at[5])
        to_scalar.start()
        to_scalar.wait()

    def stats_go(n):
        for copy in stats[n]:
            copy.start()

    def stats_come(n):
        for copy in stats[n]:
            copy.wait_recv()

    def swaps_go():
        for copy in swaps:
            copy.start()

    def swaps_come():
        for copy in swaps:
            copy.wait_recv()
        weight.wait()

    def far_go(n):
        for way in range(2):
            if n >= CUTS:
                far[way][n - CUTS + way * (CUTS // 2)].wait_recv()
            far[way][n].start()

    def pass_near():
        for way, d in ((0, 2), (1, 0)):
            for n in range(CUTS // 2):
                far[way][n + (1 - way) * (CUTS // 2)].wait_recv()
            passed[d].start()

    def pass_far():
        for way in range(2):
            for n in range(CUTS, CUTS + CUTS // 2):
                far[way][n].wait_recv()
        passed[1].start()

    def late_scores(n):
        if n == 0:
            for copy in edges[4]:
                copy.wait_recv()
            for qb in range(QB):
                window_score(qb, (LATE,))
        lax.fori_loop(n * 4, n * 4 + 4, score_late, 0)

    for n, b in enumerate([d * QB + b for b in range(QB) for d in range(NY - 1)]):
        at(n, rows[b].start)
    for p in range(PHASES):
        at(SPOT[p, 0, 3], lambda p=p: edges_go(p))
    at(6, edges_come)
    for qb in range(QB):
        at(6 + qb, lambda qb=qb: window_score(qb, range(LATE)))
    at(DONE[0], rows_come)
    bounds = [0, 2, 4, 6, 8, 10, 12, 14, 16]
    for n in range(8):
        at(DONE[0] + n, lambda n=n: lax.fori_loop(bounds[n], bounds[n + 1], score_main, 0))
    at(DONE[0] + 8, lambda: stats_go(0))
    for n, r in enumerate((1, 4, 7, 10, 13, DONE[0] + 2)):
        at(r, lambda n=n: far_go(n))
    at(DONE[0] + 8, pass_near)
    at(DONE[1] + 5, pass_far)
    for h in range(LATE):
        for i in range(QB):
            at(DONE[h + 1] + i, lambda h=h, i=i: weigh(h, i))
        at(DONE[h + 1] + QB, lambda h=h: window_weigh(h))
    at(DONE[2] + 5, lambda: stats_come(0))
    for i in range(QB):
        at(DONE[2] + 6 + i, lambda i=i: merge(0, i))
        at(DONE[3] + 5 + i, lambda i=i: merge(1, i))
        at(DONE[4], lambda i=i: merge(2, i))
    at(DONE[4], swaps_go)
    at(DONE[4] + 1, lambda: late_scores(0))
    at(DONE[4] + 2, lambda: late_scores(1))
    at(DONE[4] + 3, swaps_come, lambda: lax.fori_loop(0, TILES // 2, project, 0))
    at(DONE[4] + 4, lambda: lax.fori_loop(TILES // 2, TILES, project, 0), send_first)
    at(DONE[4] + 5, lambda: late_scores(2))
    at(DONE[4] + 6, lambda: late_scores(3), lambda: stats_go(1))
    assert max(work) < RING

    for r in range(RING):
        for way in range(2):
            rings[way][r].wait_recv()
            for n in follow.get(r, ()):
                rings[way][n].start()
        for call in work.get(r, ()):
            call()

    for i in range(QB):
        weigh(LATE, i)
    window_weigh(LATE)
    send_relayed(1)
    send_relayed(2)
    for copy in stats[1]:
        copy.wait_recv()
    for i in range(QB):
        merge(LATE, i)
        for copy in lates[i]:
            copy.start()
    come_late[mp] = att_late[QB - 1, mine, :]
    for copy in passed:
        copy.wait_recv()
    for i in range(QB - 1):
        for c in range(2):
            remote(att_late.at[i, pl.ds(0, HALF)], come_late.at[mp], late_send.at[i, c], late_recv.at[i, c],
                   {"mp": sibling}).wait_recv()
    remote(att_late.at[QB - 1, theirs], come_late.at[mp], late_send.at[QB - 1, 0], late_recv.at[QB - 1, 1 - core],
           {"mp": sibling}).wait_recv()
    sends[2].wait_recv()
    sends[3].wait_recv()

    def finish(n, carry):
        cols = pl.ds(pl.multiple_of(n * TILE, TILE), TILE)
        value = total[QB - 1, :, cols] + jnp.dot(come_late[mp], w_own[late, cols], preferred_element_type=jnp.float32)
        value += jnp.dot(come_late[sibling], w_other[late, cols], preferred_element_type=jnp.float32)
        for d in range(1, NX):
            chip = ((x + d) % NX) * 2
            pair = jnp.concatenate([come_late[chip], come_late[chip + 1]], axis=1)
            value += jnp.dot(pair, w_far[d - 1, :, cols], preferred_element_type=jnp.float32)
        value += final[0, :, cols].astype(jnp.float32) + final[1, :, cols].astype(jnp.float32)
        out_ref[:, cols] = value.astype(jnp.bfloat16)
        return carry

    lax.fori_loop(0, TILES, finish, 0)

    groups = edges + rings + far + lates + stats + [rows, numbers, swaps, sends, passed]
    groups += [c for h in range(HEADS) for c in parts[h]]
    for copies in groups:
        for copy in copies:
            copy.wait_send()


def shards(query_rows, key_rows, value_rows, out_weight, random_ids, global_ids):
    bf, f32 = jnp.bfloat16, jnp.float32
    dma = pltpu.SemaphoreType.DMA
    vmem = pltpu.VMEM
    ids = jnp.pad(random_ids, ((0, 8 - QB), (0, 128 - RAND)))
    anywhere = pl.BlockSpec(memory_space=pl.ANY)
    blocks = (QB, BLK, FEATS)
    return pl.pallas_call(
        kernel,
        name="attend_and_project",
        out_shape=jax.ShapeDtypeStruct((HALF, WIDTH), bf),
        in_specs=[anywhere] * 5 + [pl.BlockSpec(memory_space=pltpu.SMEM)],
        out_specs=pl.BlockSpec(memory_space=pltpu.VMEM),
        scratch_shapes=[
            vmem((NZ * QB, BLK, MAIN), bf),
            vmem((NZ * QB, BLK, HD), bf),
            *[vmem((NZ * QB, HD, BLK), bf)] * HEADS,
            vmem((NY * QB, BLK, FEATS), bf),
            vmem((NY, 8, 128), jnp.int32),
            pltpu.SMEM((NY, 8, 128), jnp.int32),
            vmem((2, BLK, MAIN), bf),
            vmem((2, BLK, HD), bf),
            vmem((2 * HEADS, HD, BLK), bf),
            vmem(blocks, bf),
            vmem((QB, FEATS, BLK), f32),
            vmem((QB, 2 * HEADS, BLK), f32),
            vmem((QB, HEADS, 3 * BLK, BLK), bf),
            vmem((NY * QB, HEADS, CAND * BLK, BLK), bf),
            vmem((NY * QB, FEATS, BLK), bf),
            vmem((NY * QB, 2 * HEADS, BLK), f32),
            vmem((NY * QB, 2 * HEADS, BLK), f32),
            vmem((NY - 1, QB, FEATS, BLK), bf),
            vmem((NY - 1, QB, 2 * HEADS, BLK), f32),
            vmem((NY - 1, QB, 2 * HEADS, BLK), f32),
            vmem((FEATS, WIDTH), bf),
            vmem((FEATS, WIDTH), bf),
            vmem((NX - 1, 2 * HD, WIDTH), bf),
            vmem((QB, BLK, MAIN), bf),
            vmem((QB, HALF, MAIN), bf),
            vmem((QB, BLK, HD), bf),
            vmem((2 * NX, HALF, HD), bf),
            vmem((3, HALF, WIDTH), bf),
            vmem((2, HALF, WIDTH // 2), bf),
            vmem((2, HALF, WIDTH), bf),
            vmem((QB, HALF, WIDTH), f32),
            dma((2, RING)), dma((2, RING)), dma((NY - 1, QB)), dma((NY - 1, QB)), dma((NY - 1,)), dma((NY - 1,)),
            dma((PHASES, 2)), dma((PHASES, 2)), dma((2,)), dma((7,)),
            dma((HEADS, NY - 1, QB)), dma((HEADS, NY - 1, QB)), dma((2, NY - 1)), dma((2, NY - 1)),
            dma((QB,)), dma((QB,)), dma((4,)), dma((4,)),
            dma((2, 6)), dma((2, 6)), dma((NX - 1,)), dma((NX - 1,)), dma((QB, 2)), dma((QB, 2)),
        ],
        compiler_params=pltpu.CompilerParams(
            collective_id=0, has_side_effects=True, vmem_limit_bytes=60 * MIB
        ),
        cost_estimate=pl.CostEstimate(flops=4 * 10**9, bytes_accessed=24 * MIB, transcendentals=0),
    )(
        query_rows.reshape(blocks), key_rows.reshape(blocks), value_rows.reshape(blocks),
        out_weight, ids, global_ids,
    )


def solution(mesh):
    return jax.shard_map(
        shards,
        mesh=mesh,
        in_specs=(
            P("ctx", "mp"),
            P("ctx", "mp"),
            P("ctx", "mp"),
            P("mp", None),
            P("ctx", None),
            P(),
        ),
        out_specs=P(("ctx", "mp"), None),
        check_vma=False,
    )
```

```python
import math

import jax
import jax.numpy as jnp
from jax import lax
from jax.experimental import pallas as pl
from jax.experimental.pallas import tpu as pltpu
from jax.sharding import PartitionSpec as P

HD = 128
BLK = 128
RAND = 3
GLOB = 2
CAND = GLOB + RAND
NZ = 8
NY = 4
NX = 4
HEADS = 4
QB = 4
FEATS = HEADS * HD
WIDTH = 4096
HALF = BLK // 2
TILE = 512
SCALE = 1.0 / math.sqrt(HD)
LOW = -1e30
MESH = pl.DeviceIdType.MESH
NT = (((1,), (1,)), ((), ()))
PHASES = 2 * HEADS
LATE = HEADS - 1
MAIN = LATE * HD
CUTS = 4
CUT = HD // CUTS
TILES = WIDTH // TILE
MIDDLE = WIDTH // 2
MIB = 1024 * 1024


def ring_order():
    order = [(0, 0), (2, 0), (0, 1), (1, 0), (0, 2), (1, 1), (0, 3), (1, 2), (2, 1), (1, 3)]
    for p in range(2, PHASES - 1):
        order += [(p + 1, 0), (p, 2), (p + 1, 1), (p, 3)]
    order += [(PHASES - 1, 2), (PHASES - 1, 3)]
    return [(p, back, j) for p, back in order for j in range(1 if back == 3 else 2)]


ORDER = ring_order()
RING = len(ORDER)
SPOT = {item: n for n, item in enumerate(ORDER)}
DONE = [SPOT[p, 3, 0] for p in range(PHASES)]


def followers():
    follow, last = {}, -1
    for n, (p, back, j) in enumerate(ORDER):
        if back > 0:
            last = max(last, SPOT[p, back - 1, j])
        follow.setdefault(last, []).append(n)
    return follow


def kernel(
    q_ref, k_ref, v_ref, w_ref, ids_ref, glob_ref, out_ref,
    k_col0, k_col1, k_col2, k_col3, v_col0, v_col1, v_col2, v_col3, q_row0, q_row1, q_row2, q_row3,
    id_row, id_s, k_edge, v_edge, v_own, acc, w_stat, w_probs,
    probs, part, p_stat, got, got_stat, w_own, w_other, w_far,
    att, att_other, att_late, come_late, sent, relay, final, total,
    ring_send, ring_recv, row_send, row_recv, id_send, id_recv, edge_send, edge_recv, w_sem, local_sem,
    part_send, part_recv, stat_send, stat_recv, att_send, att_recv, x_send, x_recv,
    far_send, far_recv, pass_send, pass_recv, late_send, late_recv,
):
    me, mp = lax.axis_index("ctx"), lax.axis_index("mp")
    z, y, x, core = me // NY, me % NY, mp // 2, mp % 2
    count = NZ * NY
    sibling = mp + 1 - 2 * core
    up, down = (z + 1) % NZ, (z + NZ - 1) % NZ
    right, left = ((x + 1) % NX) * 2 + core, ((x + NX - 1) % NX) * 2 + core
    order = [(x + d) % NX for d in (2, 1, 3, 0)]
    v_cols = (v_col0, v_col1, v_col2, v_col3)
    k_cols = (k_col0, k_col1, k_col2, k_col3)
    q_rows = (q_row0, q_row1, q_row2, q_row3)
    main, late = pl.ds(0, MAIN), pl.ds(MAIN, HD)

    def head(h):
        return pl.ds(h * HD, HD)

    own_keys, own_rows = pl.ds(z * QB, QB), pl.ds(y * QB, QB)
    local = [
        pltpu.make_async_copy(v_ref, v_own, local_sem.at[0]),
        pltpu.make_async_copy(ids_ref, id_row.at[y], local_sem.at[1]),
        pltpu.make_async_copy(w_ref, w_own, local_sem.at[2]),
    ]
    k_local = [pltpu.make_async_copy(k_ref.at[:, :, head(h)], k_cols[h].at[own_keys], local_sem.at[4 + h])
               for h in range(HEADS)]
    q_local = [pltpu.make_async_copy(q_ref.at[:, :, head(h)], q_rows[h].at[own_rows], local_sem.at[8 + h])
               for h in range(HEADS)]
    for k_copy, q_copy in zip(k_local, q_local):
        local += [k_copy, q_copy]
    for copy in local:
        copy.start()

    barrier = pltpu.get_barrier_semaphore()
    peers = [{"ctx": up * NY + y}, {"ctx": down * NY + y}]
    peers += [{"ctx": z * NY + (y + d) % NY} for d in range(1, NY)]
    peers += [{"mp": sibling}] + [{"mp": ((x + d) % NX) * 2 + c} for d in range(1, NX) for c in range(2)]
    for peer in peers:
        pl.semaphore_signal(barrier, inc=1, device_id=peer, device_id_type=MESH)
    pl.semaphore_wait(barrier, len(peers))

    def remote(src, dst, send, recv, peer):
        return pltpu.make_async_remote_copy(
            src_ref=src, dst_ref=dst, send_sem=send, recv_sem=recv, device_id=peer, device_id_type=MESH
        )

    def ring(way, n):
        p, back, j = ORDER[n]
        sign = 1 if way == 0 else -1
        peer = {"ctx": (up if way == 0 else down) * NY + y}
        sems = (ring_send.at[way, n], ring_recv.at[way, n])
        piece = 2 * ((j + way) % 2)
        span = pl.ds(((z + NZ - sign * back) % NZ) * QB + piece, 2)
        if p % 2:
            ref = v_cols[p // 2]
            return remote(ref.at[span], ref.at[span], *sems, peer)
        ref = k_cols[p // 2]
        src = k_ref.at[pl.ds(piece, 2), :, head(p // 2)] if back == 0 else ref.at[span]
        return remote(src, ref.at[span], *sems, peer)

    rings = [[ring(way, n) for n in range(RING)] for way in range(2)]
    follow = followers()
    for n in follow[-1]:
        rings[0][n].start()
        rings[1][n].start()

    above = jnp.where(y < NY - 1, z, down) * QB + QB - 1
    below = jnp.where(y > 0, z, up) * QB
    next_y, last_y = {"ctx": z * NY + (y + 1) % NY}, {"ctx": z * NY + (y + NY - 1) % NY}
    edges = []
    for p in range(PHASES):
        source, target = (v_cols[p // 2], v_edge) if p % 2 else (k_cols[p // 2], k_edge)
        spots = (p // 2 * 2, p // 2 * 2 + 1)
        edges.append([
            remote(source.at[above], target.at[spots[0]], edge_send.at[p, 0], edge_recv.at[p, 0], next_y),
            remote(source.at[below], target.at[spots[1]], edge_send.at[p, 1], edge_recv.at[p, 1], last_y),
        ])
    numbers, rows = [], [[] for h in range(HEADS)]
    for d in range(1, NY):
        peer = {"ctx": z * NY + (y + d) % NY}
        numbers.append(remote(ids_ref, id_row.at[y], id_send.at[d - 1], id_recv.at[d - 1], peer))
        for h in range(HEADS):
            rows[h].append(remote(q_ref.at[:, :, head(h)], q_rows[h].at[own_rows],
                                  row_send.at[d - 1, h], row_recv.at[d - 1, h], peer))
    for copy in rows[0]:
        copy.start()
    for copy in numbers:
        copy.start()
    weight = remote(w_ref, w_other, w_sem.at[0], w_sem.at[1], {"mp": sibling})
    weight.start()

    local[0].wait()

    def turn(h):
        for b in range(QB):
            v_cols[h][z * QB + b] = v_own[b, :, head(h)].T

    turn(0)

    def window_score(h):
        row = lax.broadcasted_iota(jnp.int32, (3 * BLK, 1), 0)
        for qb in range(QB):
            first = jnp.where(me + qb == 0, BLK, 0)
            last = jnp.where(me * QB + qb == count * QB - 1, 2 * BLK, 3 * BLK)
            live = (row >= first) & (row < last)
            keys = [k_edge[2 * h] if qb == 0 else k_cols[h][z * QB + qb - 1]]
            keys.append(k_cols[h][z * QB + qb])
            keys.append(k_edge[2 * h + 1] if qb == QB - 1 else k_cols[h][z * QB + qb + 1])
            s = lax.dot_general(jnp.concatenate(keys, axis=0), q_rows[h][y * QB + qb], NT,
                                preferred_element_type=jnp.float32) * SCALE
            s = jnp.where(live, s, LOW)
            top = jnp.max(s, axis=0, keepdims=True)
            p = jnp.exp(s - top).astype(jnp.bfloat16)
            w_stat[qb, pl.ds(h, 1), :] = top
            w_stat[qb, pl.ds(HEADS + h, 1), :] = jnp.sum(p.astype(jnp.float32), axis=0, keepdims=True)
            w_probs[qb, h] = p

    def window_weigh(h):
        for copy in edges[2 * h + 1]:
            copy.wait_recv()
        for qb in range(QB):
            values = [v_edge[2 * h] if qb == 0 else v_cols[h][z * QB + qb - 1]]
            values.append(v_cols[h][z * QB + qb])
            values.append(v_edge[2 * h + 1] if qb == QB - 1 else v_cols[h][z * QB + qb + 1])
            acc[qb, pl.ds(h * HD, HD), :] = jnp.dot(
                jnp.concatenate(values, axis=1), w_probs[qb, h], preferred_element_type=jnp.float32)

    def candidates(t):
        blocks = [glob_ref[j] for j in range(GLOB)]
        blocks += [id_s[lax.div(t, QB), lax.rem(t, QB), j] for j in range(RAND)]
        spots = [lax.div(block, NY * QB) * QB + lax.rem(block, QB) for block in blocks]
        return blocks, spots

    def score(h):
        def one(t, carry):
            blocks, spots = candidates(t)
            bias = [jnp.where(lax.rem(lax.div(block, QB), NY) == y, 0.0, LOW) for block in blocks]
            keys = jnp.concatenate([k_cols[h][spot] for spot in spots], axis=0)
            s = lax.dot_general(keys, q_rows[h][t], NT, preferred_element_type=jnp.float32)
            s = jnp.concatenate([s[j * BLK:(j + 1) * BLK] * SCALE + bias[j] for j in range(CAND)], axis=0)
            top = jnp.max(s, axis=0, keepdims=True)
            p = jnp.exp(s - top).astype(jnp.bfloat16)
            p_stat[h, t, pl.ds(0, 1), :] = top
            p_stat[h, t, pl.ds(1, 1), :] = jnp.sum(p.astype(jnp.float32), axis=0, keepdims=True)
            probs[t, h] = p
            return carry

        return one

    stats = [[] for h in range(HEADS)]
    for d in range(1, NY):
        to = (y + d) % NY
        for h in range(HEADS):
            stats[h].append(remote(p_stat.at[h, pl.ds(to * QB, QB)], got_stat.at[h, d - 1], stat_send.at[h, d - 1],
                                   stat_recv.at[h, d - 1], {"ctx": z * NY + to}))

    def returns(h, i):
        span = pl.ds(h * HD, HD)
        copies = []
        for d in (2, 1, 3):
            to = (y + d) % NY
            copies.append(remote(part.at[to * QB + order[i], span], got.at[d - 1, order[i], span],
                                 part_send.at[h, d - 1, i], part_recv.at[h, d - 1, i], {"ctx": z * NY + to}))
        return copies

    parts = [[returns(h, i) for i in range(QB)] for h in range(HEADS)]

    def weigh(h, i):
        def one(to, carry):
            t = to * QB + order[i]
            spots = candidates(t)[1]
            values = jnp.concatenate([v_cols[h][spot] for spot in spots], axis=1)
            out = jnp.dot(values, probs[t, h], preferred_element_type=jnp.float32)
            out = out / p_stat[h, t, pl.ds(1, 1), :]
            part[t, pl.ds(h * HD, HD), :] = out.astype(jnp.bfloat16)
            return carry

        lax.fori_loop(0, NY, one, 0)
        for copy in parts[h][i]:
            copy.start()

    def merge(h, i):
        for copy in parts[h][i]:
            copy.wait_recv()
        qb = order[i]
        cols = pl.ds(h * HD, HD)
        first, second = pl.ds(0, 1), pl.ds(1, 1)
        tops = [w_stat[qb, pl.ds(h, 1), :], p_stat[h, y * QB + qb, first, :]]
        tops += [got_stat[h, s, qb, first, :] for s in range(NY - 1)]
        sums = [w_stat[qb, pl.ds(HEADS + h, 1), :], p_stat[h, y * QB + qb, second, :]]
        sums += [got_stat[h, s, qb, second, :] for s in range(NY - 1)]
        best = tops[0]
        for top in tops[1:]:
            best = jnp.maximum(best, top)
        scales = [jnp.exp(top - best) for top in tops]
        weights = [scale * total_of for scale, total_of in zip(scales, sums)]
        low = weights[0] + weights[1] + weights[2] + weights[3] + weights[4]
        value = acc[qb, cols, :] * (scales[0] / low)
        value += part[y * QB + qb, cols, :].astype(jnp.float32) * (weights[1] / low)
        for s in range(NY - 1):
            value += got[s, qb, cols, :].astype(jnp.float32) * (weights[s + 2] / low)
        if h == LATE:
            att_late[i] = value.T.astype(jnp.bfloat16)
        else:
            att[i, :, cols] = value.T.astype(jnp.bfloat16)

    mine = pl.ds(pl.multiple_of(core * HALF, HALF), HALF)
    theirs = pl.ds(pl.multiple_of((1 - core) * HALF, HALF), HALF)
    swaps = [remote(att.at[i, theirs], att_other.at[i], att_send.at[i], att_recv.at[i], {"mp": sibling})
             for i in range(QB)]

    def project(group):
        def one(n, carry):
            cols = pl.ds(pl.multiple_of(n * TILE, TILE), TILE)
            own = jnp.concatenate([att[i, mine, :] for i in group], axis=0)
            other = jnp.concatenate([att_other[i] for i in group], axis=0)
            value = jnp.dot(own, w_own[main, cols], preferred_element_type=jnp.float32)
            value += jnp.dot(other, w_other[main, cols], preferred_element_type=jnp.float32)
            for m, i in enumerate(group):
                total[i, :, cols] = value[m * HALF:(m + 1) * HALF]
            return carry

        for i in group:
            swaps[i].wait_recv()
        lax.fori_loop(0, TILES, one, 0)

    far = [[], []]
    for way, peer in enumerate(({"mp": right}, {"mp": left})):
        from_d, to_d = (2, 0)[way], (2, 0)[way]
        for c in range(CUTS):
            rows_of = pl.ds(pl.multiple_of(core * HD + c * CUT, CUT), CUT)
            far[way].append(remote(w_ref.at[pl.ds(MAIN + c * CUT, CUT)], w_far.at[to_d, rows_of],
                                   far_send.at[way, c], far_recv.at[way, c], peer))
        for n in range(CUTS // 2):
            c = n + way * (CUTS // 2)
            rows_of = pl.ds(pl.multiple_of(core * HD + c * CUT, CUT), CUT)
            far[way].append(remote(w_far.at[from_d, rows_of], w_far.at[1, rows_of],
                                   far_send.at[way, CUTS + n], far_recv.at[way, CUTS + n], peer))
    own_half = pl.ds(pl.multiple_of(core * HD, HD), HD)
    passed = [remote(w_far.at[d, own_half], w_far.at[d, own_half], pass_send.at[d], pass_recv.at[d], {"mp": sibling})
              for d in range(NX - 1)]

    lates = []
    for i, qb in enumerate(order):
        lates.append([])
        for c in range(2):
            if i < QB - 1:
                lates[i].append(remote(att_late.at[i, pl.ds(c * HALF, HALF)], come_late.at[mp],
                                       late_send.at[i, c], late_recv.at[i, core], {"mp": qb * 2 + c}))
    lates[QB - 1].append(remote(att_late.at[QB - 1, theirs], come_late.at[mp],
                                late_send.at[QB - 1, 0], late_recv.at[QB - 1, core], {"mp": sibling}))

    sends = [remote(sent.at[0, :, pl.ds(s * MIDDLE, MIDDLE)], relay.at[s], x_send.at[s], x_recv.at[s], {"mp": peer})
             for s, peer in enumerate((right, left))]
    for n in range(2):
        for i, peer in ((1, right), (2, left)):
            side = pl.ds(((i + n) % 2) * MIDDLE, MIDDLE)
            sends.append(remote(sent.at[i, :, side], final.at[i - 1, :, side],
                                x_send.at[1 + 2 * n + i], x_recv.at[1 + 2 * n + i], {"mp": peer}))

    def send_first():
        sent[0] = total[0].astype(jnp.bfloat16)
        sends[0].start()
        sends[1].start()

    def send_direct():
        for i in (1, 2):
            there = pl.ds((i % 2) * MIDDLE, MIDDLE)
            sent[i, :, there] = total[i, :, there].astype(jnp.bfloat16)
            sends[1 + i].start()

    def send_relayed(i):
        sends[i - 1].wait_recv()
        here = pl.ds((i - 1) * MIDDLE, MIDDLE)
        sent[i, :, here] = (total[i, :, here] + relay[i - 1].astype(jnp.float32)).astype(jnp.bfloat16)
        sends[3 + i].start()

    def weights_come():
        weight.wait()
        local[2].wait()

    work = {}

    def at(r, *calls):
        work.setdefault(r, []).extend(calls)

    def edges_go(p):
        if p % 2 == 0:
            k_local[p // 2].wait()
        for copy in edges[p]:
            copy.start()

    def rows_come(h):
        q_local[h].wait()
        for copy in rows[h] + edges[2 * h]:
            copy.wait_recv()
        if h == 0:
            local[1].wait()
            for copy in numbers:
                copy.wait_recv()
            to_scalar = pltpu.make_async_copy(id_row, id_s, local_sem.at[3])
            to_scalar.start()
            to_scalar.wait()

    def stats_go(h):
        for copy in stats[h]:
            copy.start()

    def stats_come(h):
        for copy in stats[h]:
            copy.wait_recv()

    def merge_swap(i):
        merge(LATE - 1, i)
        swaps[i].start()

    def far_go(n):
        for way in range(2):
            if n >= CUTS:
                far[way][n - CUTS + way * (CUTS // 2)].wait_recv()
            far[way][n].start()

    def pass_near():
        for way, d in ((0, 2), (1, 0)):
            for n in range(CUTS // 2):
                far[way][n + (1 - way) * (CUTS // 2)].wait_recv()
            passed[d].start()

    def pass_far():
        for way in range(2):
            for n in range(CUTS, CUTS + CUTS // 2):
                far[way][n].wait_recv()
        passed[1].start()

    for h, r in ((1, 2), (2, 14), (3, 26)):
        for d in range(NY - 1):
            at(r + d, rows[h][d].start)
    for p in range(PHASES):
        at(SPOT[p, 0, 1], lambda p=p: edges_go(p))
    for n, r in enumerate((1, 5, 9, 13, 18, 22)):
        at(r, lambda n=n: far_go(n))
    at(25, pass_near)
    at(31, pass_far)
    for h in range(LATE):
        k, v = DONE[2 * h], DONE[2 * h + 1]
        at(k, lambda h=h: rows_come(h), lambda h=h: window_score(h))
        for n in range(4):
            at(k + 1 + n, lambda h=h, n=n: lax.fori_loop(4 * n, 4 * n + 4, score(h), 0))
        at(k + 5, lambda h=h: stats_go(h))
        for i in range(QB):
            at(v + i // (2 if h == LATE - 1 else 1), lambda h=h, i=i: weigh(h, i))
        at(v + (2 if h == LATE - 1 else QB), lambda h=h: window_weigh(h))
    for h in range(LATE - 1):
        at(DONE[2 * h + 2] + 5, lambda h=h: stats_come(h), lambda h=h: merge(h, 0), lambda h=h: merge(h, 1))
        at(DONE[2 * h + 2] + 6, lambda h=h: merge(h, 2), lambda h=h: merge(h, 3))
    for h in range(1, HEADS):
        at(2 * h, lambda h=h: turn(h))
    v, k = DONE[2 * LATE - 1], DONE[2 * LATE]
    at(v + 3, lambda: stats_come(LATE - 1), lambda: merge_swap(0))
    at(v + 4, weights_come, lambda: project((0,)), send_first)
    at(v + 5, lambda: merge_swap(1), lambda: merge_swap(2), lambda: merge_swap(3))
    at(v + 6, lambda: project((1, 2, 3)), send_direct)
    at(k, lambda: rows_come(LATE), lambda: window_score(LATE), lambda: lax.fori_loop(0, 5, score(LATE), 0))
    at(k + 1, lambda: lax.fori_loop(5, 10, score(LATE), 0))
    at(k + 2, lambda: lax.fori_loop(10, 16, score(LATE), 0), lambda: stats_go(LATE))
    assert max(work) < RING

    for r in range(RING):
        for way in range(2):
            rings[way][r].wait_recv()
            for n in follow.get(r, ()):
                rings[way][n].start()
        for call in work.get(r, ()):
            call()

    for i in range(QB):
        weigh(LATE, i)
    send_relayed(1)
    send_relayed(2)
    window_weigh(LATE)
    stats_come(LATE)
    for i in range(QB):
        merge(LATE, i)
        for copy in lates[i]:
            copy.start()
    come_late[mp] = att_late[QB - 1, mine, :]
    for copy in passed:
        copy.wait_recv()
    for i in range(QB - 1):
        for c in range(2):
            remote(att_late.at[i, pl.ds(0, HALF)], come_late.at[mp], late_send.at[i, c], late_recv.at[i, c],
                   {"mp": sibling}).wait_recv()
    remote(att_late.at[QB - 1, theirs], come_late.at[mp], late_send.at[QB - 1, 0], late_recv.at[QB - 1, 1 - core],
           {"mp": sibling}).wait_recv()
    for copy in sends[2:]:
        copy.wait_recv()

    def finish(n, carry):
        cols = pl.ds(pl.multiple_of(n * TILE, TILE), TILE)
        value = total[QB - 1, :, cols] + jnp.dot(come_late[mp], w_own[late, cols], preferred_element_type=jnp.float32)
        value += jnp.dot(come_late[sibling], w_other[late, cols], preferred_element_type=jnp.float32)
        for d in range(1, NX):
            chip = ((x + d) % NX) * 2
            pair = jnp.concatenate([come_late[chip], come_late[chip + 1]], axis=1)
            value += jnp.dot(pair, w_far[d - 1, :, cols], preferred_element_type=jnp.float32)
        value += final[0, :, cols].astype(jnp.float32) + final[1, :, cols].astype(jnp.float32)
        out_ref[:, cols] = value.astype(jnp.bfloat16)
        return carry

    lax.fori_loop(0, TILES, finish, 0)

    groups = edges + rings + far + lates + stats + rows + [numbers, swaps, sends, passed]
    groups += [c for h in range(HEADS) for c in parts[h]]
    for copies in groups:
        for copy in copies:
            copy.wait_send()


def shards(query_rows, key_rows, value_rows, out_weight, random_ids, global_ids):
    bf, f32 = jnp.bfloat16, jnp.float32
    dma = pltpu.SemaphoreType.DMA
    vmem = pltpu.VMEM
    ids = jnp.pad(random_ids, ((0, 8 - QB), (0, 128 - RAND)))
    anywhere = pl.BlockSpec(memory_space=pl.ANY)
    blocks = (QB, BLK, FEATS)
    return pl.pallas_call(
        kernel,
        name="attend_and_project",
        out_shape=jax.ShapeDtypeStruct((HALF, WIDTH), bf),
        in_specs=[anywhere] * 5 + [pl.BlockSpec(memory_space=pltpu.SMEM)],
        out_specs=pl.BlockSpec(memory_space=pltpu.VMEM),
        scratch_shapes=[
            *[vmem((NZ * QB, BLK, HD), bf)] * HEADS,
            *[vmem((NZ * QB, HD, BLK), bf)] * HEADS,
            *[vmem((NY * QB, BLK, HD), bf)] * HEADS,
            vmem((NY, 8, 128), jnp.int32),
            pltpu.SMEM((NY, 8, 128), jnp.int32),
            vmem((2 * HEADS, BLK, HD), bf),
            vmem((2 * HEADS, HD, BLK), bf),
            vmem(blocks, bf),
            vmem((QB, FEATS, BLK), f32),
            vmem((QB, 2 * HEADS, BLK), f32),
            vmem((QB, HEADS, 3 * BLK, BLK), bf),
            vmem((NY * QB, HEADS, CAND * BLK, BLK), bf),
            vmem((NY * QB, FEATS, BLK), bf),
            vmem((HEADS, NY * QB, 8, BLK), f32),
            vmem((NY - 1, QB, FEATS, BLK), bf),
            vmem((HEADS, NY - 1, QB, 8, BLK), f32),
            vmem((FEATS, WIDTH), bf),
            vmem((FEATS, WIDTH), bf),
            vmem((NX - 1, 2 * HD, WIDTH), bf),
            vmem((QB, BLK, MAIN), bf),
            vmem((QB, HALF, MAIN), bf),
            vmem((QB, BLK, HD), bf),
            vmem((2 * NX, HALF, HD), bf),
            vmem((3, HALF, WIDTH), bf),
            vmem((2, HALF, WIDTH // 2), bf),
            vmem((2, HALF, WIDTH), bf),
            vmem((QB, HALF, WIDTH), f32),
            dma((2, RING)), dma((2, RING)), dma((NY - 1, HEADS)), dma((NY - 1, HEADS)), dma((NY - 1,)), dma((NY - 1,)),
            dma((PHASES, 2)), dma((PHASES, 2)), dma((2,)), dma((12,)),
            dma((HEADS, NY - 1, QB)), dma((HEADS, NY - 1, QB)), dma((HEADS, NY - 1)), dma((HEADS, NY - 1)),
            dma((QB,)), dma((QB,)), dma((6,)), dma((6,)),
            dma((2, 6)), dma((2, 6)), dma((NX - 1,)), dma((NX - 1,)), dma((QB, 2)), dma((QB, 2)),
        ],
        compiler_params=pltpu.CompilerParams(
            collective_id=0, has_side_effects=True, vmem_limit_bytes=60 * MIB
        ),
        cost_estimate=pl.CostEstimate(flops=4 * 10**9, bytes_accessed=24 * MIB, transcendentals=0),
    )(
        query_rows.reshape(blocks), key_rows.reshape(blocks), value_rows.reshape(blocks),
        out_weight, ids, global_ids,
    )


def solution(mesh):
    return jax.shard_map(
        shards,
        mesh=mesh,
        in_specs=(
            P("ctx", "mp"),
            P("ctx", "mp"),
            P("ctx", "mp"),
            P("mp", None),
            P("ctx", None),
            P(),
        ),
        out_specs=P(("ctx", "mp"), None),
        check_vma=False,
    )
```

```python
import math

import jax
import jax.numpy as jnp
from jax import lax
from jax.experimental import pallas as pl
from jax.experimental.pallas import tpu as pltpu
from jax.sharding import PartitionSpec as P

HD = 128
BLK = 128
RAND = 3
GLOB = 2
CAND = GLOB + RAND
NZ = 8
NY = 4
NX = 4
HEADS = 4
QB = 4
FEATS = HEADS * HD
WIDTH = 4096
HALF = BLK // 2
TILE = 512
SCALE = 1.0 / math.sqrt(HD)
LOW = -1e30
MESH = pl.DeviceIdType.MESH
NT = (((1,), (1,)), ((), ()))
PHASES = 2 * HEADS
LATE = HEADS - 1
MAIN = LATE * HD
CUTS = 4
CUT = HD // CUTS
TILES = WIDTH // TILE
MIDDLE = WIDTH // 2
MIB = 1024 * 1024


def ring_order():
    order = [(0, 0), (2, 0), (0, 1), (1, 0), (0, 2), (1, 1), (0, 3), (1, 2), (2, 1), (1, 3)]
    for p in range(2, PHASES - 1):
        order += [(p + 1, 0), (p, 2), (p + 1, 1), (p, 3)]
    order += [(PHASES - 1, 2), (PHASES - 1, 3)]
    return [(p, back, j) for p, back in order for j in range(1 if back == 3 else 2)]


ORDER = ring_order()
RING = len(ORDER)
SPOT = {item: n for n, item in enumerate(ORDER)}
DONE = [SPOT[p, 3, 0] for p in range(PHASES)]


def followers():
    follow, last = {}, -1
    for n, (p, back, j) in enumerate(ORDER):
        if back > 0:
            last = max(last, SPOT[p, back - 1, j])
        follow.setdefault(last, []).append(n)
    return follow


def kernel(
    q_ref, k_ref, v_ref, w_ref, ids_ref, glob_ref, out_ref,
    k_col0, k_col1, k_col2, k_col3, v_col0, v_col1, v_col2, v_col3, q_row0, q_row1, q_row2, q_row3,
    id_row, id_s, k_edge, v_edge, v_own, acc, w_stat, w_probs,
    probs, part, p_stat, got, got_stat, w_own, w_other, w_far,
    att, att_other, att_late, come_late, sent, relay, final, total,
    ring_send, ring_recv, row_send, row_recv, id_send, id_recv, edge_send, edge_recv, w_sem, local_sem,
    part_send, part_recv, stat_send, stat_recv, att_send, att_recv, x_send, x_recv,
    far_send, far_recv, pass_send, pass_recv, late_send, late_recv,
):
    me, mp = lax.axis_index("ctx"), lax.axis_index("mp")
    z, y, x, core = me // NY, me % NY, mp // 2, mp % 2
    count = NZ * NY
    sibling = mp + 1 - 2 * core
    up, down = (z + 1) % NZ, (z + NZ - 1) % NZ
    right, left = ((x + 1) % NX) * 2 + core, ((x + NX - 1) % NX) * 2 + core
    order = [(x + d) % NX for d in (2, 1, 3, 0)]
    v_cols = (v_col0, v_col1, v_col2, v_col3)
    k_cols = (k_col0, k_col1, k_col2, k_col3)
    q_rows = (q_row0, q_row1, q_row2, q_row3)
    main, late = pl.ds(0, MAIN), pl.ds(MAIN, HD)

    def head(h):
        return pl.ds(h * HD, HD)

    own_keys, own_rows = pl.ds(z * QB, QB), pl.ds(y * QB, QB)
    local = [
        pltpu.make_async_copy(v_ref, v_own, local_sem.at[0]),
        pltpu.make_async_copy(ids_ref, id_row.at[y], local_sem.at[1]),
        pltpu.make_async_copy(w_ref, w_own, local_sem.at[2]),
    ]
    k_local = [pltpu.make_async_copy(k_ref.at[:, :, head(h)], k_cols[h].at[own_keys], local_sem.at[4 + h])
               for h in range(HEADS)]
    q_local = [pltpu.make_async_copy(q_ref.at[:, :, head(h)], q_rows[h].at[own_rows], local_sem.at[8 + h])
               for h in range(HEADS)]
    for k_copy, q_copy in zip(k_local, q_local):
        local += [k_copy, q_copy]
    for copy in local:
        copy.start()

    barrier = pltpu.get_barrier_semaphore()
    peers = [{"ctx": up * NY + y}, {"ctx": down * NY + y}]
    peers += [{"ctx": z * NY + (y + d) % NY} for d in range(1, NY)]
    peers += [{"mp": sibling}] + [{"mp": ((x + d) % NX) * 2 + c} for d in range(1, NX) for c in range(2)]
    for peer in peers:
        pl.semaphore_signal(barrier, inc=1, device_id=peer, device_id_type=MESH)
    pl.semaphore_wait(barrier, len(peers))

    def remote(src, dst, send, recv, peer):
        return pltpu.make_async_remote_copy(
            src_ref=src, dst_ref=dst, send_sem=send, recv_sem=recv, device_id=peer, device_id_type=MESH
        )

    def ring(way, n):
        p, back, j = ORDER[n]
        sign = 1 if way == 0 else -1
        peer = {"ctx": (up if way == 0 else down) * NY + y}
        sems = (ring_send.at[way, n], ring_recv.at[way, n])
        piece = 2 * ((j + way) % 2)
        span = pl.ds(((z + NZ - sign * back) % NZ) * QB + piece, 2)
        if p % 2:
            ref = v_cols[p // 2]
            return remote(ref.at[span], ref.at[span], *sems, peer)
        ref = k_cols[p // 2]
        src = k_ref.at[pl.ds(piece, 2), :, head(p // 2)] if back == 0 else ref.at[span]
        return remote(src, ref.at[span], *sems, peer)

    rings = [[ring(way, n) for n in range(RING)] for way in range(2)]
    follow = followers()
    for n in follow[-1]:
        rings[0][n].start()
        rings[1][n].start()

    above = jnp.where(y < NY - 1, z, down) * QB + QB - 1
    below = jnp.where(y > 0, z, up) * QB
    next_y, last_y = {"ctx": z * NY + (y + 1) % NY}, {"ctx": z * NY + (y + NY - 1) % NY}
    edges = []
    for p in range(PHASES):
        source, target = (v_cols[p // 2], v_edge) if p % 2 else (k_cols[p // 2], k_edge)
        spots = (p // 2 * 2, p // 2 * 2 + 1)
        edges.append([
            remote(source.at[above], target.at[spots[0]], edge_send.at[p, 0], edge_recv.at[p, 0], next_y),
            remote(source.at[below], target.at[spots[1]], edge_send.at[p, 1], edge_recv.at[p, 1], last_y),
        ])
    numbers, rows = [], [[] for h in range(HEADS)]
    for d in range(1, NY):
        peer = {"ctx": z * NY + (y + d) % NY}
        numbers.append(remote(ids_ref, id_row.at[y], id_send.at[d - 1], id_recv.at[d - 1], peer))
        for h in range(HEADS):
            rows[h].append(remote(q_ref.at[:, :, head(h)], q_rows[h].at[own_rows],
                                  row_send.at[d - 1, h], row_recv.at[d - 1, h], peer))
    for copy in rows[0]:
        copy.start()
    for copy in numbers:
        copy.start()
    weight = remote(w_ref, w_other, w_sem.at[0], w_sem.at[1], {"mp": sibling})
    weight.start()

    local[0].wait()

    def turn(h):
        for b in range(QB):
            v_cols[h][z * QB + b] = v_own[b, :, head(h)].T

    turn(0)

    def window_score(h):
        row = lax.broadcasted_iota(jnp.int32, (3 * BLK, 1), 0)
        for qb in range(QB):
            first = jnp.where(me + qb == 0, BLK, 0)
            last = jnp.where(me * QB + qb == count * QB - 1, 2 * BLK, 3 * BLK)
            live = (row >= first) & (row < last)
            keys = [k_edge[2 * h] if qb == 0 else k_cols[h][z * QB + qb - 1]]
            keys.append(k_cols[h][z * QB + qb])
            keys.append(k_edge[2 * h + 1] if qb == QB - 1 else k_cols[h][z * QB + qb + 1])
            s = lax.dot_general(jnp.concatenate(keys, axis=0), q_rows[h][y * QB + qb], NT,
                                preferred_element_type=jnp.float32) * SCALE
            s = jnp.where(live, s, LOW)
            top = jnp.max(s, axis=0, keepdims=True)
            p = jnp.exp(s - top).astype(jnp.bfloat16)
            w_stat[qb, pl.ds(h, 1), :] = top
            w_stat[qb, pl.ds(HEADS + h, 1), :] = jnp.sum(p.astype(jnp.float32), axis=0, keepdims=True)
            w_probs[qb, h] = p

    def window_weigh(h):
        for copy in edges[2 * h + 1]:
            copy.wait_recv()
        for qb in range(QB):
            values = [v_edge[2 * h] if qb == 0 else v_cols[h][z * QB + qb - 1]]
            values.append(v_cols[h][z * QB + qb])
            values.append(v_edge[2 * h + 1] if qb == QB - 1 else v_cols[h][z * QB + qb + 1])
            acc[qb, pl.ds(h * HD, HD), :] = jnp.dot(
                jnp.concatenate(values, axis=1), w_probs[qb, h], preferred_element_type=jnp.float32)

    def candidates(t):
        blocks = [glob_ref[j] for j in range(GLOB)]
        blocks += [id_s[lax.div(t, QB), lax.rem(t, QB), j] for j in range(RAND)]
        spots = [lax.div(block, NY * QB) * QB + lax.rem(block, QB) for block in blocks]
        return blocks, spots

    def score(h):
        def one(t, carry):
            blocks, spots = candidates(t)
            bias = [jnp.where(lax.rem(lax.div(block, QB), NY) == y, 0.0, LOW) for block in blocks]
            keys = jnp.concatenate([k_cols[h][spot] for spot in spots], axis=0)
            s = lax.dot_general(keys, q_rows[h][t], NT, preferred_element_type=jnp.float32)
            s = jnp.concatenate([s[j * BLK:(j + 1) * BLK] * SCALE + bias[j] for j in range(CAND)], axis=0)
            top = jnp.max(s, axis=0, keepdims=True)
            p = jnp.exp(s - top).astype(jnp.bfloat16)
            p_stat[h, t, pl.ds(0, 1), :] = top
            p_stat[h, t, pl.ds(1, 1), :] = jnp.sum(p.astype(jnp.float32), axis=0, keepdims=True)
            probs[t, h] = p
            return carry

        return one

    stats = [[] for h in range(HEADS)]
    for d in range(1, NY):
        to = (y + d) % NY
        for h in range(HEADS):
            stats[h].append(remote(p_stat.at[h, pl.ds(to * QB, QB)], got_stat.at[h, d - 1], stat_send.at[h, d - 1],
                                   stat_recv.at[h, d - 1], {"ctx": z * NY + to}))

    def returns(h, i):
        span = pl.ds(h * HD, HD)
        copies = []
        for d in (2, 1, 3):
            to = (y + d) % NY
            copies.append(remote(part.at[to * QB + order[i], span], got.at[d - 1, order[i], span],
                                 part_send.at[h, d - 1, i], part_recv.at[h, d - 1, i], {"ctx": z * NY + to}))
        return copies

    parts = [[returns(h, i) for i in range(QB)] for h in range(HEADS)]

    def weigh(h, i):
        def one(to, carry):
            t = to * QB + order[i]
            spots = candidates(t)[1]
            values = jnp.concatenate([v_cols[h][spot] for spot in spots], axis=1)
            out = jnp.dot(values, probs[t, h], preferred_element_type=jnp.float32)
            out = out / p_stat[h, t, pl.ds(1, 1), :]
            part[t, pl.ds(h * HD, HD), :] = out.astype(jnp.bfloat16)
            return carry

        lax.fori_loop(0, NY, one, 0, unroll=True)
        for copy in parts[h][i]:
            copy.start()

    def merge(h, i):
        for copy in parts[h][i]:
            copy.wait_recv()
        qb = order[i]
        cols = pl.ds(h * HD, HD)
        first, second = pl.ds(0, 1), pl.ds(1, 1)
        tops = [w_stat[qb, pl.ds(h, 1), :], p_stat[h, y * QB + qb, first, :]]
        tops += [got_stat[h, s, qb, first, :] for s in range(NY - 1)]
        sums = [w_stat[qb, pl.ds(HEADS + h, 1), :], p_stat[h, y * QB + qb, second, :]]
        sums += [got_stat[h, s, qb, second, :] for s in range(NY - 1)]
        best = tops[0]
        for top in tops[1:]:
            best = jnp.maximum(best, top)
        scales = [jnp.exp(top - best) for top in tops]
        weights = [scale * total_of for scale, total_of in zip(scales, sums)]
        low = weights[0] + weights[1] + weights[2] + weights[3] + weights[4]
        value = acc[qb, cols, :] * (scales[0] / low)
        value += part[y * QB + qb, cols, :].astype(jnp.float32) * (weights[1] / low)
        for s in range(NY - 1):
            value += got[s, qb, cols, :].astype(jnp.float32) * (weights[s + 2] / low)
        if h == LATE:
            att_late[i] = value.T.astype(jnp.bfloat16)
        else:
            att[i, :, cols] = value.T.astype(jnp.bfloat16)

    mine = pl.ds(pl.multiple_of(core * HALF, HALF), HALF)
    theirs = pl.ds(pl.multiple_of((1 - core) * HALF, HALF), HALF)
    swaps = [remote(att.at[i, theirs], att_other.at[i], att_send.at[i], att_recv.at[i], {"mp": sibling})
             for i in range(QB)]

    def project(group):
        def one(n, carry):
            cols = pl.ds(pl.multiple_of(n * TILE, TILE), TILE)
            own = jnp.concatenate([att[i, mine, :] for i in group], axis=0)
            other = jnp.concatenate([att_other[i] for i in group], axis=0)
            value = jnp.dot(own, w_own[main, cols], preferred_element_type=jnp.float32)
            value += jnp.dot(other, w_other[main, cols], preferred_element_type=jnp.float32)
            for m, i in enumerate(group):
                total[i, :, cols] = value[m * HALF:(m + 1) * HALF]
            return carry

        for i in group:
            swaps[i].wait_recv()
        lax.fori_loop(0, TILES, one, 0, unroll=True)

    far = [[], []]
    for way, peer in enumerate(({"mp": right}, {"mp": left})):
        from_d, to_d = (2, 0)[way], (2, 0)[way]
        for c in range(CUTS):
            rows_of = pl.ds(pl.multiple_of(core * HD + c * CUT, CUT), CUT)
            far[way].append(remote(w_ref.at[pl.ds(MAIN + c * CUT, CUT)], w_far.at[to_d, rows_of],
                                   far_send.at[way, c], far_recv.at[way, c], peer))
        for n in range(CUTS // 2):
            c = n + way * (CUTS // 2)
            rows_of = pl.ds(pl.multiple_of(core * HD + c * CUT, CUT), CUT)
            far[way].append(remote(w_far.at[from_d, rows_of], w_far.at[1, rows_of],
                                   far_send.at[way, CUTS + n], far_recv.at[way, CUTS + n], peer))
    own_half = pl.ds(pl.multiple_of(core * HD, HD), HD)
    passed = [remote(w_far.at[d, own_half], w_far.at[d, own_half], pass_send.at[d], pass_recv.at[d], {"mp": sibling})
              for d in range(NX - 1)]

    lates = []
    for i, qb in enumerate(order):
        lates.append([])
        for c in range(2):
            if i < QB - 1:
                lates[i].append(remote(att_late.at[i, pl.ds(c * HALF, HALF)], come_late.at[mp],
                                       late_send.at[i, c], late_recv.at[i, core], {"mp": qb * 2 + c}))
    lates[QB - 1].append(remote(att_late.at[QB - 1, theirs], come_late.at[mp],
                                late_send.at[QB - 1, 0], late_recv.at[QB - 1, core], {"mp": sibling}))

    sends = [remote(sent.at[0, :, pl.ds(s * MIDDLE, MIDDLE)], relay.at[s], x_send.at[s], x_recv.at[s], {"mp": peer})
             for s, peer in enumerate((right, left))]
    for n in range(2):
        for i, peer in ((1, right), (2, left)):
            side = pl.ds(((i + n) % 2) * MIDDLE, MIDDLE)
            sends.append(remote(sent.at[i, :, side], final.at[i - 1, :, side],
                                x_send.at[1 + 2 * n + i], x_recv.at[1 + 2 * n + i], {"mp": peer}))

    def send_first():
        sent[0] = total[0].astype(jnp.bfloat16)
        sends[0].start()
        sends[1].start()

    def send_direct():
        for i in (1, 2):
            there = pl.ds((i % 2) * MIDDLE, MIDDLE)
            sent[i, :, there] = total[i, :, there].astype(jnp.bfloat16)
            sends[1 + i].start()

    def send_relayed(i):
        sends[i - 1].wait_recv()
        here = pl.ds((i - 1) * MIDDLE, MIDDLE)
        sent[i, :, here] = (total[i, :, here] + relay[i - 1].astype(jnp.float32)).astype(jnp.bfloat16)
        sends[3 + i].start()

    def weights_come():
        weight.wait()
        local[2].wait()

    work = {}

    def at(r, *calls):
        work.setdefault(r, []).extend(calls)

    def edges_go(p):
        if p % 2 == 0:
            k_local[p // 2].wait()
        for copy in edges[p]:
            copy.start()

    def rows_come(h):
        q_local[h].wait()
        for copy in rows[h] + edges[2 * h]:
            copy.wait_recv()
        if h == 0:
            local[1].wait()
            for copy in numbers:
                copy.wait_recv()
            to_scalar = pltpu.make_async_copy(id_row, id_s, local_sem.at[3])
            to_scalar.start()
            to_scalar.wait()

    def stats_go(h):
        for copy in stats[h]:
            copy.start()

    def stats_come(h):
        for copy in stats[h]:
            copy.wait_recv()

    def merge_swap(i):
        merge(LATE - 1, i)
        swaps[i].start()

    def far_go(n):
        for way in range(2):
            if n >= CUTS:
                far[way][n - CUTS + way * (CUTS // 2)].wait_recv()
            far[way][n].start()

    def pass_near():
        for way, d in ((0, 2), (1, 0)):
            for n in range(CUTS // 2):
                far[way][n + (1 - way) * (CUTS // 2)].wait_recv()
            passed[d].start()

    def pass_far():
        for way in range(2):
            for n in range(CUTS, CUTS + CUTS // 2):
                far[way][n].wait_recv()
        passed[1].start()

    for h, r in ((1, 2), (2, 14), (3, 26)):
        for d in range(NY - 1):
            at(r + d, rows[h][d].start)
    for p in range(PHASES):
        at(SPOT[p, 0, 1], lambda p=p: edges_go(p))
    for n, r in enumerate((1, 5, 9, 13, 18, 22)):
        at(r, lambda n=n: far_go(n))
    at(25, pass_near)
    at(31, pass_far)
    for h in range(LATE):
        k, v = DONE[2 * h], DONE[2 * h + 1]
        at(k, lambda h=h: rows_come(h), lambda h=h: window_score(h))
        for n in range(4):
            at(k + 1 + n, lambda h=h, n=n: lax.fori_loop(4 * n, 4 * n + 4, score(h), 0, unroll=True))
        at(k + 5, lambda h=h: stats_go(h))
        for i in range(QB):
            at(v + i // (2 if h == LATE - 1 else 1), lambda h=h, i=i: weigh(h, i))
        at(v + (1 if h == LATE - 1 else QB), lambda h=h: window_weigh(h))
    for h in range(LATE - 1):
        at(DONE[2 * h + 2] + 5, lambda h=h: stats_come(h), lambda h=h: merge(h, 0), lambda h=h: merge(h, 1))
        at(DONE[2 * h + 2] + 6, lambda h=h: merge(h, 2), lambda h=h: merge(h, 3))
    for h in range(1, HEADS):
        at(2 * h, lambda h=h: turn(h))
    v, k = DONE[2 * LATE - 1], DONE[2 * LATE]
    at(v + 2, lambda: stats_come(LATE - 1), lambda: merge_swap(0))
    at(v + 3, weights_come, lambda: project((0,)), send_first)
    at(v + 4, lambda: merge_swap(1), lambda: merge_swap(2), lambda: merge_swap(3))
    at(v + 5, lambda: project((1, 2, 3)), send_direct)
    at(k, lambda: rows_come(LATE), lambda: window_score(LATE), lambda: lax.fori_loop(0, 5, score(LATE), 0, unroll=True))
    at(k + 1, lambda: lax.fori_loop(5, 10, score(LATE), 0, unroll=True))
    at(k + 2, lambda: lax.fori_loop(10, 16, score(LATE), 0, unroll=True), lambda: stats_go(LATE))
    assert max(work) < RING

    for r in range(RING):
        for way in range(2):
            rings[way][r].wait_recv()
            for n in follow.get(r, ()):
                rings[way][n].start()
        for call in work.get(r, ()):
            call()

    for i in range(QB):
        weigh(LATE, i)
    send_relayed(1)
    send_relayed(2)
    window_weigh(LATE)
    stats_come(LATE)
    for i in range(QB):
        merge(LATE, i)
        for copy in lates[i]:
            copy.start()
    come_late[mp] = att_late[QB - 1, mine, :]
    for copy in passed:
        copy.wait_recv()
    for i in range(QB - 1):
        for c in range(2):
            remote(att_late.at[i, pl.ds(0, HALF)], come_late.at[mp], late_send.at[i, c], late_recv.at[i, c],
                   {"mp": sibling}).wait_recv()
    remote(att_late.at[QB - 1, theirs], come_late.at[mp], late_send.at[QB - 1, 0], late_recv.at[QB - 1, 1 - core],
           {"mp": sibling}).wait_recv()

    def finish(n, carry):
        cols = pl.ds(pl.multiple_of(n * TILE, TILE), TILE)
        value = total[QB - 1, :, cols] + jnp.dot(come_late[mp], w_own[late, cols], preferred_element_type=jnp.float32)
        value += jnp.dot(come_late[sibling], w_other[late, cols], preferred_element_type=jnp.float32)
        for d in range(1, NX):
            chip = ((x + d) % NX) * 2
            pair = jnp.concatenate([come_late[chip], come_late[chip + 1]], axis=1)
            value += jnp.dot(pair, w_far[d - 1, :, cols], preferred_element_type=jnp.float32)
        total[QB - 1, :, cols] = value
        return carry

    lax.fori_loop(0, TILES, finish, 0, unroll=True)
    for copy in sends[2:]:
        copy.wait_recv()

    def add(n, carry):
        cols = pl.ds(pl.multiple_of(n * TILE, TILE), TILE)
        value = final[0, :, cols].astype(jnp.float32) + final[1, :, cols].astype(jnp.float32)
        out_ref[:, cols] = (total[QB - 1, :, cols] + value).astype(jnp.bfloat16)
        return carry

    lax.fori_loop(0, TILES, add, 0, unroll=True)

    groups = edges + rings + far + lates + stats + rows + [numbers, swaps, sends, passed]
    groups += [c for h in range(HEADS) for c in parts[h]]
    for copies in groups:
        for copy in copies:
            copy.wait_send()


def shards(query_rows, key_rows, value_rows, out_weight, random_ids, global_ids):
    bf, f32 = jnp.bfloat16, jnp.float32
    dma = pltpu.SemaphoreType.DMA
    vmem = pltpu.VMEM
    ids = jnp.pad(random_ids, ((0, 8 - QB), (0, 128 - RAND)))
    anywhere = pl.BlockSpec(memory_space=pl.ANY)
    blocks = (QB, BLK, FEATS)
    return pl.pallas_call(
        kernel,
        name="attend_and_project",
        out_shape=jax.ShapeDtypeStruct((HALF, WIDTH), bf),
        in_specs=[anywhere] * 5 + [pl.BlockSpec(memory_space=pltpu.SMEM)],
        out_specs=pl.BlockSpec(memory_space=pltpu.VMEM),
        scratch_shapes=[
            *[vmem((NZ * QB, BLK, HD), bf)] * HEADS,
            *[vmem((NZ * QB, HD, BLK), bf)] * HEADS,
            *[vmem((NY * QB, BLK, HD), bf)] * HEADS,
            vmem((NY, 8, 128), jnp.int32),
            pltpu.SMEM((NY, 8, 128), jnp.int32),
            vmem((2 * HEADS, BLK, HD), bf),
            vmem((2 * HEADS, HD, BLK), bf),
            vmem(blocks, bf),
            vmem((QB, FEATS, BLK), f32),
            vmem((QB, 2 * HEADS, BLK), f32),
            vmem((QB, HEADS, 3 * BLK, BLK), bf),
            vmem((NY * QB, HEADS, CAND * BLK, BLK), bf),
            vmem((NY * QB, FEATS, BLK), bf),
            vmem((HEADS, NY * QB, 8, BLK), f32),
            vmem((NY - 1, QB, FEATS, BLK), bf),
            vmem((HEADS, NY - 1, QB, 8, BLK), f32),
            vmem((FEATS, WIDTH), bf),
            vmem((FEATS, WIDTH), bf),
            vmem((NX - 1, 2 * HD, WIDTH), bf),
            vmem((QB, BLK, MAIN), bf),
            vmem((QB, HALF, MAIN), bf),
            vmem((QB, BLK, HD), bf),
            vmem((2 * NX, HALF, HD), bf),
            vmem((3, HALF, WIDTH), bf),
            vmem((2, HALF, WIDTH // 2), bf),
            vmem((2, HALF, WIDTH), bf),
            vmem((QB, HALF, WIDTH), f32),
            dma((2, RING)), dma((2, RING)), dma((NY - 1, HEADS)), dma((NY - 1, HEADS)), dma((NY - 1,)), dma((NY - 1,)),
            dma((PHASES, 2)), dma((PHASES, 2)), dma((2,)), dma((12,)),
            dma((HEADS, NY - 1, QB)), dma((HEADS, NY - 1, QB)), dma((HEADS, NY - 1)), dma((HEADS, NY - 1)),
            dma((QB,)), dma((QB,)), dma((6,)), dma((6,)),
            dma((2, 6)), dma((2, 6)), dma((NX - 1,)), dma((NX - 1,)), dma((QB, 2)), dma((QB, 2)),
        ],
        compiler_params=pltpu.CompilerParams(
            collective_id=0, has_side_effects=True, vmem_limit_bytes=60 * MIB
        ),
        cost_estimate=pl.CostEstimate(flops=4 * 10**9, bytes_accessed=24 * MIB, transcendentals=0),
    )(
        query_rows.reshape(blocks), key_rows.reshape(blocks), value_rows.reshape(blocks),
        out_weight, ids, global_ids,
    )


def solution(mesh):
    return jax.shard_map(
        shards,
        mesh=mesh,
        in_specs=(
            P("ctx", "mp"),
            P("ctx", "mp"),
            P("ctx", "mp"),
            P("mp", None),
            P("ctx", None),
            P(),
        ),
        out_specs=P(("ctx", "mp"), None),
        check_vma=False,
    )
```

```python
import math

import jax
import jax.numpy as jnp
from jax import lax
from jax.experimental import pallas as pl
from jax.experimental.pallas import tpu as pltpu
from jax.sharding import PartitionSpec as P

HD = 128
BLK = 128
RAND = 3
GLOB = 2
CAND = GLOB + RAND
NZ = 8
NY = 4
NX = 4
HEADS = 4
QB = 4
FEATS = HEADS * HD
WIDTH = 4096
HALF = BLK // 2
TILE = 512
SCALE = 1.0 / math.sqrt(HD)
LOW = -1e30
MESH = pl.DeviceIdType.MESH
NT = (((1,), (1,)), ((), ()))
PHASES = 2 * HEADS
LATE = HEADS - 1
MAIN = LATE * HD
CUTS = 4
CUT = HD // CUTS
TILES = WIDTH // TILE
MIDDLE = WIDTH // 2
MIB = 1024 * 1024


def ring_order():
    order = [(0, 0), (2, 0), (0, 1), (1, 0), (0, 2), (1, 1), (0, 3), (1, 2), (2, 1), (1, 3)]
    for p in range(2, PHASES - 1):
        order += [(p + 1, 0), (p, 2), (p + 1, 1), (p, 3)]
    order += [(PHASES - 1, 2), (PHASES - 1, 3)]
    return [(p, back, j) for p, back in order for j in range(1 if back == 3 else 2)]


ORDER = ring_order()
RING = len(ORDER)
SPOT = {item: n for n, item in enumerate(ORDER)}
DONE = [SPOT[p, 3, 0] for p in range(PHASES)]


def followers():
    follow, last = {}, -1
    for n, (p, back, j) in enumerate(ORDER):
        if back > 0:
            last = max(last, SPOT[p, back - 1, j])
        follow.setdefault(last, []).append(n)
    return follow


def kernel(
    q_ref, k_ref, v_ref, w_ref, ids_ref, glob_ref, out_ref,
    k_col0, k_col1, k_col2, k_col3, v_col0, v_col1, v_col2, v_col3, q_row0, q_row1, q_row2, q_row3,
    id_row, id_s, k_edge, v_edge, v_own, acc, w_stat, w_probs,
    probs, part, p_stat, got, got_stat, w_own, w_other, w_far,
    att, att_other, att_late, come_late, sent, relay, final, total,
    ring_send, ring_recv, row_send, row_recv, id_send, id_recv, edge_send, edge_recv, w_sem, local_sem,
    part_send, part_recv, stat_send, stat_recv, att_send, att_recv, x_send, x_recv,
    far_send, far_recv, pass_send, pass_recv, late_send, late_recv,
):
    me, mp = lax.axis_index("ctx"), lax.axis_index("mp")
    z, y, x, core = me // NY, me % NY, mp // 2, mp % 2
    count = NZ * NY
    sibling = mp + 1 - 2 * core
    up, down = (z + 1) % NZ, (z + NZ - 1) % NZ
    right, left = ((x + 1) % NX) * 2 + core, ((x + NX - 1) % NX) * 2 + core
    order = [(x + d) % NX for d in (2, 1, 3, 0)]
    v_cols = (v_col0, v_col1, v_col2, v_col3)
    k_cols = (k_col0, k_col1, k_col2, k_col3)
    q_rows = (q_row0, q_row1, q_row2, q_row3)
    main, late = pl.ds(0, MAIN), pl.ds(MAIN, HD)

    def head(h):
        return pl.ds(h * HD, HD)

    own_keys, own_rows = pl.ds(z * QB, QB), pl.ds(y * QB, QB)
    local = [
        pltpu.make_async_copy(v_ref, v_own, local_sem.at[0]),
        pltpu.make_async_copy(ids_ref, id_row.at[y], local_sem.at[1]),
        pltpu.make_async_copy(w_ref, w_own, local_sem.at[2]),
    ]
    k_local = [pltpu.make_async_copy(k_ref.at[:, :, head(h)], k_cols[h].at[own_keys], local_sem.at[4 + h])
               for h in range(HEADS)]
    q_local = [pltpu.make_async_copy(q_ref.at[:, :, head(h)], q_rows[h].at[own_rows], local_sem.at[8 + h])
               for h in range(HEADS)]
    for k_copy, q_copy in zip(k_local, q_local):
        local += [k_copy, q_copy]
    for copy in local:
        copy.start()

    barrier = pltpu.get_barrier_semaphore()
    peers = [{"ctx": up * NY + y}, {"ctx": down * NY + y}]
    peers += [{"ctx": z * NY + (y + d) % NY} for d in range(1, NY)]
    peers += [{"mp": sibling}] + [{"mp": ((x + d) % NX) * 2 + c} for d in range(1, NX) for c in range(2)]
    for peer in peers:
        pl.semaphore_signal(barrier, inc=1, device_id=peer, device_id_type=MESH)
    pl.semaphore_wait(barrier, len(peers))

    def remote(src, dst, send, recv, peer):
        return pltpu.make_async_remote_copy(
            src_ref=src, dst_ref=dst, send_sem=send, recv_sem=recv, device_id=peer, device_id_type=MESH
        )

    def ring(way, n):
        p, back, j = ORDER[n]
        sign = 1 if way == 0 else -1
        peer = {"ctx": (up if way == 0 else down) * NY + y}
        sems = (ring_send.at[way, n], ring_recv.at[way, n])
        piece = 2 * ((j + way) % 2)
        span = pl.ds(((z + NZ - sign * back) % NZ) * QB + piece, 2)
        if p % 2:
            ref = v_cols[p // 2]
            return remote(ref.at[span], ref.at[span], *sems, peer)
        ref = k_cols[p // 2]
        src = k_ref.at[pl.ds(piece, 2), :, head(p // 2)] if back == 0 else ref.at[span]
        return remote(src, ref.at[span], *sems, peer)

    rings = [[ring(way, n) for n in range(RING)] for way in range(2)]
    follow = followers()
    for n in follow[-1]:
        rings[0][n].start()
        rings[1][n].start()

    above = jnp.where(y < NY - 1, z, down) * QB + QB - 1
    below = jnp.where(y > 0, z, up) * QB
    next_y, last_y = {"ctx": z * NY + (y + 1) % NY}, {"ctx": z * NY + (y + NY - 1) % NY}
    edges = []
    for p in range(PHASES):
        source, target = (v_cols[p // 2], v_edge) if p % 2 else (k_cols[p // 2], k_edge)
        spots = (p // 2 * 2, p // 2 * 2 + 1)
        edges.append([
            remote(source.at[above], target.at[spots[0]], edge_send.at[p, 0], edge_recv.at[p, 0], next_y),
            remote(source.at[below], target.at[spots[1]], edge_send.at[p, 1], edge_recv.at[p, 1], last_y),
        ])
    numbers, rows = [], [[] for h in range(HEADS)]
    for d in range(1, NY):
        peer = {"ctx": z * NY + (y + d) % NY}
        numbers.append(remote(ids_ref, id_row.at[y], id_send.at[d - 1], id_recv.at[d - 1], peer))
        for h in range(HEADS):
            rows[h].append(remote(q_ref.at[:, :, head(h)], q_rows[h].at[own_rows],
                                  row_send.at[d - 1, h], row_recv.at[d - 1, h], peer))
    for copy in rows[0]:
        copy.start()
    for copy in numbers:
        copy.start()
    weight = remote(w_ref, w_other, w_sem.at[0], w_sem.at[1], {"mp": sibling})
    weight.start()

    local[0].wait()

    def turn(h):
        for b in range(QB):
            v_cols[h][z * QB + b] = v_own[b, :, head(h)].T

    turn(0)

    def window_score(h):
        row = lax.broadcasted_iota(jnp.int32, (3 * BLK, 1), 0)
        for qb in range(QB):
            first = jnp.where(me + qb == 0, BLK, 0)
            last = jnp.where(me * QB + qb == count * QB - 1, 2 * BLK, 3 * BLK)
            live = (row >= first) & (row < last)
            keys = [k_edge[2 * h] if qb == 0 else k_cols[h][z * QB + qb - 1]]
            keys.append(k_cols[h][z * QB + qb])
            keys.append(k_edge[2 * h + 1] if qb == QB - 1 else k_cols[h][z * QB + qb + 1])
            s = lax.dot_general(jnp.concatenate(keys, axis=0), q_rows[h][y * QB + qb], NT,
                                preferred_element_type=jnp.float32) * SCALE
            s = jnp.where(live, s, LOW)
            top = jnp.max(s, axis=0, keepdims=True)
            p = jnp.exp(s - top).astype(jnp.bfloat16)
            w_stat[qb, pl.ds(h, 1), :] = top
            w_stat[qb, pl.ds(HEADS + h, 1), :] = jnp.sum(p.astype(jnp.float32), axis=0, keepdims=True)
            w_probs[qb, h] = p

    def window_weigh(h):
        for copy in edges[2 * h + 1]:
            copy.wait_recv()
        for qb in range(QB):
            values = [v_edge[2 * h] if qb == 0 else v_cols[h][z * QB + qb - 1]]
            values.append(v_cols[h][z * QB + qb])
            values.append(v_edge[2 * h + 1] if qb == QB - 1 else v_cols[h][z * QB + qb + 1])
            acc[qb, pl.ds(h * HD, HD), :] = jnp.dot(
                jnp.concatenate(values, axis=1), w_probs[qb, h], preferred_element_type=jnp.float32)

    def candidates(t):
        blocks = [glob_ref[j] for j in range(GLOB)]
        blocks += [id_s[lax.div(t, QB), lax.rem(t, QB), j] for j in range(RAND)]
        spots = [lax.div(block, NY * QB) * QB + lax.rem(block, QB) for block in blocks]
        return blocks, spots

    def score(h):
        def one(t, carry):
            blocks, spots = candidates(t)
            bias = [jnp.where(lax.rem(lax.div(block, QB), NY) == y, 0.0, LOW) for block in blocks]
            keys = jnp.concatenate([k_cols[h][spot] for spot in spots], axis=0)
            s = lax.dot_general(keys, q_rows[h][t], NT, preferred_element_type=jnp.float32)
            s = jnp.concatenate([s[j * BLK:(j + 1) * BLK] * SCALE + bias[j] for j in range(CAND)], axis=0)
            top = jnp.max(s, axis=0, keepdims=True)
            p = jnp.exp(s - top).astype(jnp.bfloat16)
            p_stat[h, t, pl.ds(0, 1), :] = top
            p_stat[h, t, pl.ds(1, 1), :] = jnp.sum(p.astype(jnp.float32), axis=0, keepdims=True)
            probs[t, h] = p
            return carry

        return one

    stats = [[] for h in range(HEADS)]
    for d in range(1, NY):
        to = (y + d) % NY
        for h in range(HEADS):
            stats[h].append(remote(p_stat.at[h, pl.ds(to * QB, QB)], got_stat.at[h, d - 1], stat_send.at[h, d - 1],
                                   stat_recv.at[h, d - 1], {"ctx": z * NY + to}))

    def returns(h, i):
        span = pl.ds(h * HD, HD)
        copies = []
        for d in (2, 1, 3):
            to = (y + d) % NY
            copies.append(remote(part.at[to * QB + order[i], span], got.at[d - 1, order[i], span],
                                 part_send.at[h, d - 1, i], part_recv.at[h, d - 1, i], {"ctx": z * NY + to}))
        return copies

    parts = [[returns(h, i) for i in range(QB)] for h in range(HEADS)]

    def weigh(h, i):
        def one(to, carry):
            t = to * QB + order[i]
            spots = candidates(t)[1]
            values = jnp.concatenate([v_cols[h][spot] for spot in spots], axis=1)
            out = jnp.dot(values, probs[t, h], preferred_element_type=jnp.float32)
            out = out / p_stat[h, t, pl.ds(1, 1), :]
            part[t, pl.ds(h * HD, HD), :] = out.astype(jnp.bfloat16)
            return carry

        lax.fori_loop(0, NY, one, 0, unroll=True)
        for copy in parts[h][i]:
            copy.start()

    def merge(h, i):
        for copy in parts[h][i]:
            copy.wait_recv()
        qb = order[i]
        cols = pl.ds(h * HD, HD)
        first, second = pl.ds(0, 1), pl.ds(1, 1)
        tops = [w_stat[qb, pl.ds(h, 1), :], p_stat[h, y * QB + qb, first, :]]
        tops += [got_stat[h, s, qb, first, :] for s in range(NY - 1)]
        sums = [w_stat[qb, pl.ds(HEADS + h, 1), :], p_stat[h, y * QB + qb, second, :]]
        sums += [got_stat[h, s, qb, second, :] for s in range(NY - 1)]
        best = tops[0]
        for top in tops[1:]:
            best = jnp.maximum(best, top)
        scales = [jnp.exp(top - best) for top in tops]
        weights = [scale * total_of for scale, total_of in zip(scales, sums)]
        low = weights[0] + weights[1] + weights[2] + weights[3] + weights[4]
        value = acc[qb, cols, :] * (scales[0] / low)
        value += part[y * QB + qb, cols, :].astype(jnp.float32) * (weights[1] / low)
        for s in range(NY - 1):
            value += got[s, qb, cols, :].astype(jnp.float32) * (weights[s + 2] / low)
        if h == LATE:
            att_late[i] = value.T.astype(jnp.bfloat16)
        else:
            att[i, :, cols] = value.T.astype(jnp.bfloat16)

    mine = pl.ds(pl.multiple_of(core * HALF, HALF), HALF)
    theirs = pl.ds(pl.multiple_of((1 - core) * HALF, HALF), HALF)
    swaps = [remote(att.at[i, theirs], att_other.at[i], att_send.at[i], att_recv.at[i], {"mp": sibling})
             for i in range(QB)]

    def project(group):
        def one(n, carry):
            cols = pl.ds(pl.multiple_of(n * TILE, TILE), TILE)
            own = jnp.concatenate([att[i, mine, :] for i in group], axis=0)
            other = jnp.concatenate([att_other[i] for i in group], axis=0)
            value = jnp.dot(own, w_own[main, cols], preferred_element_type=jnp.float32)
            value += jnp.dot(other, w_other[main, cols], preferred_element_type=jnp.float32)
            for m, i in enumerate(group):
                total[i, :, cols] = value[m * HALF:(m + 1) * HALF]
            return carry

        for i in group:
            swaps[i].wait_recv()
        lax.fori_loop(0, TILES, one, 0, unroll=True)

    far = [[], []]
    for way, peer in enumerate(({"mp": right}, {"mp": left})):
        from_d, to_d = (2, 0)[way], (2, 0)[way]
        for c in range(CUTS):
            rows_of = pl.ds(pl.multiple_of(core * HD + c * CUT, CUT), CUT)
            far[way].append(remote(w_ref.at[pl.ds(MAIN + c * CUT, CUT)], w_far.at[to_d, rows_of],
                                   far_send.at[way, c], far_recv.at[way, c], peer))
        for n in range(CUTS // 2):
            c = n + way * (CUTS // 2)
            rows_of = pl.ds(pl.multiple_of(core * HD + c * CUT, CUT), CUT)
            far[way].append(remote(w_far.at[from_d, rows_of], w_far.at[1, rows_of],
                                   far_send.at[way, CUTS + n], far_recv.at[way, CUTS + n], peer))
    own_half = pl.ds(pl.multiple_of(core * HD, HD), HD)
    passed = [remote(w_far.at[d, own_half], w_far.at[d, own_half], pass_send.at[d], pass_recv.at[d], {"mp": sibling})
              for d in range(NX - 1)]

    lates = []
    for i, qb in enumerate(order):
        lates.append([])
        for c in range(2):
            if i < QB - 1:
                lates[i].append(remote(att_late.at[i, pl.ds(c * HALF, HALF)], come_late.at[mp],
                                       late_send.at[i, c], late_recv.at[i, core], {"mp": qb * 2 + c}))
    lates[QB - 1].append(remote(att_late.at[QB - 1, theirs], come_late.at[mp],
                                late_send.at[QB - 1, 0], late_recv.at[QB - 1, core], {"mp": sibling}))

    sends = [remote(sent.at[0, :, pl.ds(s * MIDDLE, MIDDLE)], relay.at[s], x_send.at[s], x_recv.at[s], {"mp": peer})
             for s, peer in enumerate((right, left))]
    for n in range(2):
        for i, peer in ((1, right), (2, left)):
            side = pl.ds(((i + n) % 2) * MIDDLE, MIDDLE)
            sends.append(remote(sent.at[i, :, side], final.at[i - 1, :, side],
                                x_send.at[1 + 2 * n + i], x_recv.at[1 + 2 * n + i], {"mp": peer}))

    def send_first():
        sent[0] = total[0].astype(jnp.bfloat16)
        sends[0].start()
        sends[1].start()

    def send_direct():
        for i in (1, 2):
            there = pl.ds((i % 2) * MIDDLE, MIDDLE)
            sent[i, :, there] = total[i, :, there].astype(jnp.bfloat16)
            sends[1 + i].start()

    def send_relayed(i):
        sends[i - 1].wait_recv()
        here = pl.ds((i - 1) * MIDDLE, MIDDLE)
        sent[i, :, here] = (total[i, :, here] + relay[i - 1].astype(jnp.float32)).astype(jnp.bfloat16)
        sends[3 + i].start()

    def weights_come():
        weight.wait()
        local[2].wait()

    work = {}

    def at(r, *calls):
        work.setdefault(r, []).extend(calls)

    def edges_go(p):
        if p % 2 == 0:
            k_local[p // 2].wait()
        for copy in edges[p]:
            copy.start()

    def rows_come(h):
        q_local[h].wait()
        for copy in rows[h] + edges[2 * h]:
            copy.wait_recv()
        if h == 0:
            local[1].wait()
            for copy in numbers:
                copy.wait_recv()
            to_scalar = pltpu.make_async_copy(id_row, id_s, local_sem.at[3])
            to_scalar.start()
            to_scalar.wait()

    def stats_go(h):
        for copy in stats[h]:
            copy.start()

    def stats_come(h):
        for copy in stats[h]:
            copy.wait_recv()

    def merge_swap(i):
        merge(LATE - 1, i)
        swaps[i].start()

    def far_go(n):
        for way in range(2):
            if n >= CUTS:
                far[way][n - CUTS + way * (CUTS // 2)].wait_recv()
            far[way][n].start()

    def pass_near():
        for way, d in ((0, 2), (1, 0)):
            for n in range(CUTS // 2):
                far[way][n + (1 - way) * (CUTS // 2)].wait_recv()
            passed[d].start()

    def pass_far():
        for way in range(2):
            for n in range(CUTS, CUTS + CUTS // 2):
                far[way][n].wait_recv()
        passed[1].start()

    for h, r in ((1, 2), (2, 14), (3, 26)):
        for d in range(NY - 1):
            at(r + d, rows[h][d].start)
    for p in range(PHASES):
        at(SPOT[p, 0, 1], lambda p=p: edges_go(p))
    for n, r in enumerate((1, 5, 9, 13, 18, 22)):
        at(r, lambda n=n: far_go(n))
    at(25, pass_near)
    at(31, pass_far)
    for h in range(LATE):
        k, v = DONE[2 * h], DONE[2 * h + 1]
        at(k, lambda h=h: rows_come(h), lambda h=h: window_score(h))
        bounds = (0, 4, 8, 12, 16) if h == 0 else (0, 3, 6, 9, 12, 14, 16)
        for n in range(len(bounds) - 1):
            at(k + 1 + n, lambda h=h, low=bounds[n], high=bounds[n + 1]: lax.fori_loop(low, high, score(h), 0, unroll=True))
        at(k + len(bounds) - 1, lambda h=h: stats_go(h))
        for i in range(QB):
            at(v + i // (2 if h == LATE - 1 else 1), lambda h=h, i=i: weigh(h, i))
        at(v + (1 if h == LATE - 1 else QB), lambda h=h: window_weigh(h))
    for h in range(LATE - 1):
        at(DONE[2 * h + 2] + 5, lambda h=h: stats_come(h), lambda h=h: merge(h, 0), lambda h=h: merge(h, 1))
        at(DONE[2 * h + 2] + 6, lambda h=h: merge(h, 2), lambda h=h: merge(h, 3))
    for h in range(1, HEADS):
        at(2 * h, lambda h=h: turn(h))
    v, k = DONE[2 * LATE - 1], DONE[2 * LATE]
    at(v + 2, lambda: stats_come(LATE - 1), lambda: merge_swap(0))
    at(v + 3, weights_come, lambda: project((0,)), send_first)
    at(v + 4, lambda: merge_swap(1), lambda: merge_swap(2), lambda: merge_swap(3))
    at(v + 5, lambda: project((1, 2, 3)), send_direct)
    at(k, lambda: rows_come(LATE), lambda: window_score(LATE), lambda: lax.fori_loop(0, 5, score(LATE), 0, unroll=True))
    at(k + 1, lambda: lax.fori_loop(5, 10, score(LATE), 0, unroll=True))
    at(k + 2, lambda: lax.fori_loop(10, 16, score(LATE), 0, unroll=True), lambda: stats_go(LATE))
    assert max(work) < RING

    for r in range(RING):
        for way in range(2):
            rings[way][r].wait_recv()
            for n in follow.get(r, ()):
                rings[way][n].start()
        for call in work.get(r, ()):
            call()

    for i in range(QB):
        weigh(LATE, i)
    send_relayed(1)
    send_relayed(2)
    window_weigh(LATE)
    stats_come(LATE)
    for i in range(QB):
        merge(LATE, i)
        for copy in lates[i]:
            copy.start()
    come_late[mp] = att_late[QB - 1, mine, :]
    for copy in passed:
        copy.wait_recv()
    for i in range(QB - 1):
        for c in range(2):
            remote(att_late.at[i, pl.ds(0, HALF)], come_late.at[mp], late_send.at[i, c], late_recv.at[i, c],
                   {"mp": sibling}).wait_recv()
    remote(att_late.at[QB - 1, theirs], come_late.at[mp], late_send.at[QB - 1, 0], late_recv.at[QB - 1, 1 - core],
           {"mp": sibling}).wait_recv()

    def finish(n, carry):
        cols = pl.ds(pl.multiple_of(n * TILE, TILE), TILE)
        value = total[QB - 1, :, cols] + jnp.dot(come_late[mp], w_own[late, cols], preferred_element_type=jnp.float32)
        value += jnp.dot(come_late[sibling], w_other[late, cols], preferred_element_type=jnp.float32)
        for d in range(1, NX):
            chip = ((x + d) % NX) * 2
            pair = jnp.concatenate([come_late[chip], come_late[chip + 1]], axis=1)
            value += jnp.dot(pair, w_far[d - 1, :, cols], preferred_element_type=jnp.float32)
        total[QB - 1, :, cols] = value
        return carry

    lax.fori_loop(0, TILES, finish, 0, unroll=True)
    for copy in sends[2:]:
        copy.wait_recv()

    def add(n, carry):
        cols = pl.ds(pl.multiple_of(n * TILE, TILE), TILE)
        value = final[0, :, cols].astype(jnp.float32) + final[1, :, cols].astype(jnp.float32)
        out_ref[:, cols] = (total[QB - 1, :, cols] + value).astype(jnp.bfloat16)
        return carry

    lax.fori_loop(0, TILES, add, 0, unroll=True)

    groups = edges + rings + far + lates + stats + rows + [numbers, swaps, sends, passed]
    groups += [c for h in range(HEADS) for c in parts[h]]
    for copies in groups:
        for copy in copies:
            copy.wait_send()


def shards(query_rows, key_rows, value_rows, out_weight, random_ids, global_ids):
    bf, f32 = jnp.bfloat16, jnp.float32
    dma = pltpu.SemaphoreType.DMA
    vmem = pltpu.VMEM
    ids = jnp.pad(random_ids, ((0, 8 - QB), (0, 128 - RAND)))
    anywhere = pl.BlockSpec(memory_space=pl.ANY)
    blocks = (QB, BLK, FEATS)
    return pl.pallas_call(
        kernel,
        name="attend_and_project",
        out_shape=jax.ShapeDtypeStruct((HALF, WIDTH), bf),
        in_specs=[anywhere] * 5 + [pl.BlockSpec(memory_space=pltpu.SMEM)],
        out_specs=pl.BlockSpec(memory_space=pltpu.VMEM),
        scratch_shapes=[
            *[vmem((NZ * QB, BLK, HD), bf)] * HEADS,
            *[vmem((NZ * QB, HD, BLK), bf)] * HEADS,
            *[vmem((NY * QB, BLK, HD), bf)] * HEADS,
            vmem((NY, 8, 128), jnp.int32),
            pltpu.SMEM((NY, 8, 128), jnp.int32),
            vmem((2 * HEADS, BLK, HD), bf),
            vmem((2 * HEADS, HD, BLK), bf),
            vmem(blocks, bf),
            vmem((QB, FEATS, BLK), f32),
            vmem((QB, 2 * HEADS, BLK), f32),
            vmem((QB, HEADS, 3 * BLK, BLK), bf),
            vmem((NY * QB, HEADS, CAND * BLK, BLK), bf),
            vmem((NY * QB, FEATS, BLK), bf),
            vmem((HEADS, NY * QB, 8, BLK), f32),
            vmem((NY - 1, QB, FEATS, BLK), bf),
            vmem((HEADS, NY - 1, QB, 8, BLK), f32),
            vmem((FEATS, WIDTH), bf),
            vmem((FEATS, WIDTH), bf),
            vmem((NX - 1, 2 * HD, WIDTH), bf),
            vmem((QB, BLK, MAIN), bf),
            vmem((QB, HALF, MAIN), bf),
            vmem((QB, BLK, HD), bf),
            vmem((2 * NX, HALF, HD), bf),
            vmem((3, HALF, WIDTH), bf),
            vmem((2, HALF, WIDTH // 2), bf),
            vmem((2, HALF, WIDTH), bf),
            vmem((QB, HALF, WIDTH), f32),
            dma((2, RING)), dma((2, RING)), dma((NY - 1, HEADS)), dma((NY - 1, HEADS)), dma((NY - 1,)), dma((NY - 1,)),
            dma((PHASES, 2)), dma((PHASES, 2)), dma((2,)), dma((12,)),
            dma((HEADS, NY - 1, QB)), dma((HEADS, NY - 1, QB)), dma((HEADS, NY - 1)), dma((HEADS, NY - 1)),
            dma((QB,)), dma((QB,)), dma((6,)), dma((6,)),
            dma((2, 6)), dma((2, 6)), dma((NX - 1,)), dma((NX - 1,)), dma((QB, 2)), dma((QB, 2)),
        ],
        compiler_params=pltpu.CompilerParams(
            collective_id=0, has_side_effects=True, vmem_limit_bytes=60 * MIB
        ),
        cost_estimate=pl.CostEstimate(flops=4 * 10**9, bytes_accessed=24 * MIB, transcendentals=0),
    )(
        query_rows.reshape(blocks), key_rows.reshape(blocks), value_rows.reshape(blocks),
        out_weight, ids, global_ids,
    )


def solution(mesh):
    return jax.shard_map(
        shards,
        mesh=mesh,
        in_specs=(
            P("ctx", "mp"),
            P("ctx", "mp"),
            P("ctx", "mp"),
            P("mp", None),
            P("ctx", None),
            P(),
        ),
        out_specs=P(("ctx", "mp"), None),
        check_vma=False,
    )
```
